256 devices in a mesh: gx: 4 (over x), gy: 8 (over z_lo, core), gz: 8 (over y, z_hi).
Axes of the slice: x: 4, y: 4, z: 8 (z_hi: 2, z_lo: 4; z = z_hi * 4 + z_lo), core: 2. Of those that a mesh axis runs over, the one named last changes fastest.
Arguments:
- source: float32 [64, 256, 1024], P('gx', 'gy', 'gz'), may hold values from -8 to 8
- conductivity: float32 [64, 256, 1024], P('gx', 'gy', 'gz'), may hold values from 0.1 to 10
Outputs:
- correction: float32 [64, 256, 1024], P('gx', 'gy', 'gz')
- residual: float32 [64, 256, 1024], P('gx', 'gy', 'gz')
The draws below stay inside these ranges and needn't reach their ends.
All inputs are finite; a program needn't handle non-finite values.
Results may differ from the reference program's by a relative error of at most 0.0001.
Values sent between devices are 32-bit elements; how exact they have to be, the bound alone decides.
A program may use at most 128 MiB of HBM per device.

```python
import math
import jax
import jax.numpy as jnp

NX = 64
NY = 256
NZ = 1024


def levels(key, extent, split, least, top_value):
    factor_of = 1.0
    for dim, shards_of in split:
        draws = jax.random.uniform(jax.random.fold_in(jax.random.fold_in(key, 6), dim), (shards_of,), jnp.float32, least / len(split), top_value / len(split))
        factor_of = factor_of * jnp.repeat(jnp.exp(draws), extent[dim] // shards_of).reshape((-1,) + (1,) * (len(extent) - 1 - dim))
    return factor_of


def bell_draw(rng, extent, deviation, limit, shards=(), dtype=jnp.bfloat16):
    array = deviation * jax.random.normal(rng, extent, jnp.float32)
    if shards:
        array = array * levels(rng, extent, shards, -0.22, 0.18)
    return jnp.clip(array, -limit, limit).astype(dtype)


def setup_inputs(seed: int = 0) -> dict:
    arg_keys = jax.random.split(jax.random.key(seed), 3)
    source = bell_draw(arg_keys[0], (NX, NY, NZ), 1.0, 8.0, ((0, 4), (1, 8), (2, 8)), jnp.float32)
    conductivity = jnp.clip(jnp.exp(math.log(10.0) - 4.6051702 * jax.random.uniform(arg_keys[1], (NX, NY, NZ), jnp.float32) ** levels(arg_keys[1], (NX, NY, NZ), ((0, 4), (1, 8), (2, 8)), -0.2, 0.2)), 0.1, 10.0)
    return {"source": source, "conductivity": conductivity}


CHEB_HIGH = 2.0
CHEB_LOW = 0.3


def restrict_sum(field):
    size_x, size_y, size_z = field.shape
    return field.reshape(size_x // 2, 2, size_y // 2, 2, size_z // 2, 2).sum(axis=(1, 3, 5))


def coarsen_mean(field):
    return restrict_sum(field) * 0.125


def prolong(field):
    return jnp.repeat(jnp.repeat(jnp.repeat(field, 2, axis=0), 2, axis=1), 2, axis=2)


def level_couplings(padded, coeff, factor):
    parts = (padded[:-2, 1:-1, 1:-1], padded[2:, 1:-1, 1:-1], padded[1:-1, :-2, 1:-1],
             padded[1:-1, 2:, 1:-1], padded[1:-1, 1:-1, :-2], padded[1:-1, 1:-1, 2:])
    couplings = tuple(factor * 0.5 * (coeff + neighbour) for neighbour in parts)
    diagonal = couplings[0]
    for extra in couplings[1:]:
        diagonal = diagonal + extra
    return couplings, diagonal


def apply_op(padded, field, couplings, diagonal):
    parts = (padded[:-2, 1:-1, 1:-1], padded[2:, 1:-1, 1:-1], padded[1:-1, :-2, 1:-1],
             padded[1:-1, 2:, 1:-1], padded[1:-1, 1:-1, :-2], padded[1:-1, 1:-1, 2:])
    neighbours = couplings[0] * parts[0]
    for index in range(1, 6):
        neighbours = neighbours + couplings[index] * parts[index]
    return diagonal * field - neighbours


def smooth(target, start, operators, sweeps, extend):
    couplings, diagonal = operators
    centre = (CHEB_HIGH + CHEB_LOW) / 2.0
    half_width = (CHEB_HIGH - CHEB_LOW) / 2.0
    sharpness = centre / half_width
    weight = 1.0 / sharpness
    if start is None:
        update = (target / diagonal) * (1.0 / centre)
        approx = update
    else:
        remain = target - apply_op(extend(start), start, couplings, diagonal)
        update = (remain / diagonal) * (1.0 / centre)
        approx = start + update
    for sweep in range(sweeps - 1):
        remain = target - apply_op(extend(approx), approx, couplings, diagonal)
        weight_new = 1.0 / (2.0 * sharpness - weight)
        update = weight_new * weight * update + (2.0 * weight_new / half_width) * (remain / diagonal)
        approx = approx + update
        weight = weight_new
    return approx


def vcycle(target, coeff, extend):
    coeff_low = coarsen_mean(coeff)
    upper = level_couplings(extend(coeff), coeff, 8.0)
    lower = level_couplings(extend(coeff_low), coeff_low, 16.0)
    approx = smooth(target, None, upper, 2, extend)
    residue = target - apply_op(extend(approx), approx, upper[0], upper[1])
    lower_fix = smooth(restrict_sum(residue), None, lower, 4, extend)
    approx = approx + prolong(lower_fix)
    return smooth(target, approx, upper, 2, extend)


def zero_extend(field):
    return jnp.pad(field, 1)


def reference(source, conductivity):
    targets = [source]
    coeffs = [conductivity]
    for level in range(3):
        targets.append(restrict_sum(targets[-1]))
        coeffs.append(coarsen_mean(coeffs[-1]))
    corrections = []
    fine_ops = None
    for level in range(3):
        operators = level_couplings(zero_extend(coeffs[level]), coeffs[level], float(2 ** level))
        if level == 0:
            fine_ops = operators
        first = smooth(targets[level], None, operators, 3, zero_extend)
        corrections.append(smooth(targets[level], first, operators, 3, zero_extend))
    summed = vcycle(targets[3], coeffs[3], zero_extend)
    for level in (2, 1, 0):
        summed = corrections[level] + prolong(summed)
    residual = source - apply_op(zero_extend(summed), summed, fine_ops[0], fine_ops[1])
    return summed, residual
```

```python
import jax
import jax.numpy as jnp
from jax import lax
from jax.experimental import pallas as pl
from jax.experimental.pallas import tpu as pltpu
from jax.sharding import PartitionSpec as P

f32 = jnp.float32
MESH = pl.DeviceIdType.MESH

CENTRE = (2.0 + 0.3) / 2.0
HALF = (2.0 - 0.3) / 2.0
SHARP = CENTRE / HALF
W0 = 1.0 / SHARP
W1 = 1.0 / (2.0 * SHARP - W0)
W2 = 1.0 / (2.0 * SHARP - W1)
W3 = 1.0 / (2.0 * SHARP - W2)
B0 = 1.0 / CENTRE
A1, B1 = W1 * W0, 2.0 * W1 / HALF
A2, B2 = W2 * W1, 2.0 * W2 / HALF
A3, B3 = W3 * W2, 2.0 * W3 / HALF

NEAR = [(dx, dy) for dx in (-1, 0, 1) for dy in (-1, 0, 1) if (dx, dy) != (0, 0)]
PLANE = [(a, b) for a in range(4) for b in range(8) if (a, b) != (0, 0)]


def lanes(rows):
    return lax.broadcasted_iota(jnp.int32, (rows, 128), 1)


def rowid(rows):
    return lax.broadcasted_iota(jnp.int32, (rows, 128), 0)


def gat(x, idx):
    return jnp.take_along_axis(x, idx, axis=1, mode="promise_in_bounds")


def roll(x, shift):
    return pltpu.roll(x, shift, 1)


def loop(lo, hi, body):
    def step(i, c):
        body(i)
        return c

    lax.fori_loop(lo, hi, step, 0)


def rem(a, n):
    return lax.rem(a, n)


class Level:
    def __init__(self, refs, planes, rows, factor, mask):
        self.K, self.R, self.CX, self.CY, self.CZ, self.ID, self.VA, self.VB = refs
        self.X, self.Y, self.h, self.mask = planes, rows, 0.5 * factor, mask

    def clear(self):
        Y = self.Y
        pad = jnp.zeros((8, 128), f32)

        def body(i):
            for ref in (self.K, self.VA, self.VB):
                ref[i, 0:8] = pad
                ref[i, 8 + Y : 16 + Y] = pad

        loop(0, self.X, body)
        full = jnp.zeros((Y, 128), f32)
        for i in (0, self.X - 1):
            for ref in (self.VA, self.VB, self.K):
                ref[i, 8 : 8 + Y] = full

    def build(self):
        Y, h, K = self.Y, self.h, self.K

        def body(i):
            k = K[i, 8 : 8 + Y]
            low = h * (k + K[i - 1, 8 : 8 + Y])
            high = h * (k + K[i + 1, 8 : 8 + Y])
            self.CX[i] = low
            self.CX[i + 1] = high
            self.CY[i] = h * (K[i, 8 : 16 + Y] + K[i, 7 : 15 + Y])
            cz = h * (k + roll(k, 1))
            self.CZ[i] = cz
            ylow = h * (k + K[i, 7 : 7 + Y])
            yhigh = h * (k + K[i, 9 : 9 + Y])
            d = low + high + ylow + yhigh + cz + roll(cz, 127)
            inv = jnp.where(self.mask(i), 1.0 / d, 0.0)
            self.ID[i] = inv
            self.VA[i, 8 : 8 + Y] = B0 * (self.R[i] * inv)

        loop(1, self.X - 1, body)

    def flux(self, V, i):
        Y = self.Y
        v = V[i, 8 : 8 + Y]
        out = self.CX[i] * (v - V[i - 1, 8 : 8 + Y])
        out = out + self.CX[i + 1] * (v - V[i + 1, 8 : 8 + Y])
        out = out + self.CY[i, 0:Y] * (v - V[i, 7 : 7 + Y])
        out = out + self.CY[i, 1 : 1 + Y] * (v - V[i, 9 : 9 + Y])
        fz = self.CZ[i] * (v - roll(v, 1))
        return v, out + (fz - roll(fz, 127))

    def step(self, src, dst, a, b, shrink, first=False):
        Y = self.Y

        def body(i):
            v, av = self.flux(src, i)
            new = v + b * (self.ID[i] * (self.R[i] - av))
            if first:
                new = new + a * v
            elif a != 0.0:
                new = new + a * (v - dst[i, 8 : 8 + Y])
            dst[i, 8 : 8 + Y] = new

        loop(1 + shrink, self.X - 1 - shrink, body)

    def smooth6(self, after=None, trim=True):
        plan = [
            (self.VA, self.VB, A1, B1, True),
            (self.VB, self.VA, A2, B2, False),
            (self.VA, self.VB, 0.0, B0, False),
            (self.VB, self.VA, A1, B1, False),
            (self.VA, self.VB, A2, B2, False),
        ]
        for n, (src, dst, a, b, first) in enumerate(plan):
            self.step(src, dst, a, b, n + 1 if trim else 0, first)
            if after is not None and n < 4:
                after(dst)


def kernel(r_in, k_in, corr_out, res_out, *s):
    (E0, E1, E23, XB, PB, RK2, T, TH, RES, HV, KH, sem_loc, e0s, e0r, e1s, e1r, gs, gr, bs, br, xs, xr, cs, cr, *lv) = s
    gx, gy, gz = lax.axis_index("gx"), lax.axis_index("gy"), lax.axis_index("gz")
    own = gx * 8 + gy

    bar = pltpu.get_barrier_semaphore()

    def peer(a, b):
        return rem(gx + a, 4), rem(gy + b, 8)

    for a, b in PLANE:
        px, py = peer(a, b)
        pl.semaphore_signal(bar, inc=1, device_id={"gx": px, "gy": py}, device_id_type=MESH)

    @pl.when(gz > 0)
    def _():
        pl.semaphore_signal(bar, inc=1, device_id={"gz": gz - 1}, device_id_type=MESH)

    @pl.when(gz < 7)
    def _():
        pl.semaphore_signal(bar, inc=1, device_id={"gz": gz + 1}, device_id_type=MESH)

    def yz(rows, ylo, ny, zlo, zown, zhi):
        y = rowid(rows) + ylo
        l = lanes(rows)
        low = jnp.where(gz > 0, 128 - zlo, 128)
        high = jnp.where(gz < 7, zown + zhi, zown)
        return (y >= 0) & (y < ny) & ((l < high) | (l >= low))

    def with_x(base, rows, x, nx):
        xv = jnp.zeros((rows, 128), jnp.int32) + x
        return base & (xv >= 0) & (xv < nx)

    def mask0(i):
        return with_x(yz(48, 32 * gy - 8, 256, 0, 128, 0), 48, 16 * gx + i - 7, 64)

    def group(rows):
        l = lanes(rows)
        g = jnp.where(l >= 84, 2, jnp.where(l >= 42, 1, 0))
        return l, g, l - 42 * g

    def masks(i):
        l, g, zz = group(48)
        y = rowid(48) + (32 * gy - 8)
        x = 10 * g + (16 * gx + i - 8)
        low = jnp.where(gz > 0, 0, 8)
        high = jnp.where(gz < 7, 42, 34)
        return (y >= 0) & (y < 256) & (x >= 0) & (x < 64) & (zz >= low) & (zz < high) & (l < 126)

    def mask1(i):
        return with_x(yz(32, 16 * gy - 8, 128, 8, 64, 8), 32, 8 * gx + i - 7, 32)

    def mask2(i):
        return with_x(yz(24, 8 * gy - 8, 64, 8, 32, 8), 24, 4 * gx + i - 7, 16)

    def mask3(i):
        return yz(32, 0, 32, 16, 16, 16)

    def mask4(i):
        return yz(16, 0, 16, 8, 8, 8)

    L0 = Level(lv[0:8], 30, 48, 1.0, mask0)
    LS = Level(lv[8:16], 12, 48, 1.0, masks)
    L1 = Level(lv[16:24], 22, 32, 2.0, mask1)
    L2 = Level(lv[24:32], 18, 24, 4.0, mask2)
    L3 = Level(lv[32:40], 10, 32, 8.0, mask3)
    L4 = Level(lv[40:48], 6, 16, 16.0, mask4)

    loc = [
        pltpu.make_async_copy(ref, E0.at[n, 7:23, 8:40], sem_loc.at[n]) for n, ref in enumerate((r_in, k_in))
    ]
    for c in loc:
        c.start()

    l32 = lanes(32)
    zero32 = jnp.zeros((32, 128), f32)

    def pack0(x, c):
        r8, k8 = roll(r_in[x], 8 * x), roll(k_in[x], 8 * x)
        here, before = (l32 >> 3) == x, (l32 >> 3) == ((x + 15) & 15)
        return (
            jnp.where(here, r8, c[0]),
            jnp.where(here, k8, c[1]),
            jnp.where(before, r8, c[2]),
            jnp.where(before, k8, c[3]),
        )

    packed = lax.fori_loop(0, 16, pack0, (zero32,) * 4)
    PB[0, 0], PB[0, 1] = packed[0], packed[1]
    PB[1, 0], PB[1, 1] = roll(packed[2], 8), roll(packed[3], 8)

    def pair(x, rows):
        l = lanes(rows)
        return gat(x, (2 * l) & 127) + gat(x, (2 * l + 1) & 127)

    l16 = lanes(16)

    def down1(x, c):
        out = []
        for ref in (r_in, k_in):
            t = (ref[2 * x, pl.ds(0, 16, stride=2)] + ref[2 * x, pl.ds(1, 16, stride=2)]) + (
                ref[2 * x + 1, pl.ds(0, 16, stride=2)] + ref[2 * x + 1, pl.ds(1, 16, stride=2)]
            )
            out.append(pair(t, 16))
        rk = jnp.where(l16 < 64, out[0], 0.125 * out[1])
        E1[7 + x, 8:24] = rk
        here = ((l16 & 63) >> 3) == x
        return (
            jnp.where(here, roll(rk, 8 * x), c[0]),
            jnp.where(here, roll(rk, (8 * x + 72) & 127), c[1]),
        )

    zero16 = jnp.zeros((16, 128), f32)
    low1, high1 = lax.fori_loop(0, 8, down1, (zero16, zero16))
    for side, val in enumerate((low1, high1)):
        PB[side, 2, 0:8] = val[0:8]
        PB[side, 2, 24:32] = val[8:16]

    l8 = lanes(8)
    zero8 = jnp.zeros((8, 128), f32)

    def down2(x, c):
        def part(p, n):
            return E1[7 + 2 * x + p, pl.ds(8 + n, 8, stride=2)]

        t = (part(0, 0) + part(0, 1)) + (part(1, 0) + part(1, 1))
        rk = pair(t, 8)
        rk = jnp.where(((l8 >> 5) & 1) == 1, 0.125 * rk, rk)
        RK2[x] = rk
        here, edge = (l8 >> 5) == x, (l8 < 64) & (((l8 & 31) >> 3) == x)
        return (
            jnp.where(here, roll(rk, 32 * x), c[0]),
            jnp.where(here, roll(rk, (32 * x + 96) & 127), c[1]),
            jnp.where(edge, roll(rk, 8 * x), c[2]),
            jnp.where(edge, roll(rk, (8 * x + 104) & 127), c[3]),
        )

    r2, k2, low2, high2 = lax.fori_loop(0, 4, down2, (zero8,) * 4)
    l4 = lanes(4)
    rk3 = []
    for x in range(2):
        t = (RK2[2 * x, pl.ds(0, 4, stride=2)] + RK2[2 * x, pl.ds(1, 4, stride=2)]) + (
            RK2[2 * x + 1, pl.ds(0, 4, stride=2)] + RK2[2 * x + 1, pl.ds(1, 4, stride=2)]
        )
        T[0:4], T[4:8] = t, t
        t = pair(T[0:8], 8)
        rk3.append(jnp.where(((l8 >> 4) & 1) == 1, 0.125 * t, t))
    m3 = jnp.where(((l8 >> 5) & 1) == 0, rk3[0], rk3[1])
    E23[own, 0], E23[own, 1], E23[own, 2] = r2, k2, m3
    RK2[0] = jnp.where(l8 < 64, low2, m3)
    RK2[1] = jnp.where(l8 < 64, high2, m3)

    for L in (L0, LS, L1, L2, L3, L4):
        L.clear()

    pl.semaphore_wait(bar, 31 + jnp.where(gz > 0, 1, 0) + jnp.where(gz < 7, 1, 0))

    def zcopies(side):
        dev = {"gz": gz - 1 if side == 0 else gz + 1}
        land = 1 - side
        pieces = [
            (PB.at[side, 0:2], XB.at[1, land, 0:2, 8:40]),
            (PB.at[side, 2, 0:8], XB.at[1, land, 2, 8:16]),
            (PB.at[side, 2, 24:32], XB.at[1, land, 2, 32:40]),
            (RK2.at[side], E23.at[own, 3 + land]),
        ]
        return [
            pltpu.make_async_remote_copy(
                src_ref=src, dst_ref=dst, send_sem=bs.at[side, n], recv_sem=br.at[side, n],
                device_id=dev, device_id_type=MESH,
            )
            for n, (src, dst) in enumerate(pieces)
        ]

    def each(cond, copies, what):
        @pl.when(cond)
        def _():
            for c in copies:
                getattr(c, what)()

    zdown, zup = zcopies(0), zcopies(1)
    each(gz > 0, zdown[::-1], "start")
    each(gz < 7, zup[::-1], "start")

    for c in loc:
        c.wait()

    def inside(dx, dy):
        return (gx + dx >= 0) & (gx + dx < 4) & (gy + dy >= 0) & (gy + dy < 8)

    SRC0X, DST0X = {-1: (7, 14), 0: (7, 23), 1: (16, 23)}, {-1: (23, 30), 0: (7, 23), 1: (0, 7)}
    SRC0Y, DST0Y = {-1: (8, 16), 0: (8, 40), 1: (32, 40)}, {-1: (40, 48), 0: (8, 40), 1: (0, 8)}
    SRC1X, DST1X = {-1: (7, 14), 0: (7, 15), 1: (8, 15)}, {-1: (15, 22), 0: (7, 15), 1: (0, 7)}
    SRC1Y, DST1Y = {-1: (8, 16), 0: (8, 24), 1: (16, 24)}, {-1: (24, 32), 0: (8, 24), 1: (0, 8)}

    def sl(pairs):
        return pl.ds(pairs[0], pairs[1] - pairs[0])

    def near_copies(make):
        return [(inside(dx, dy), inside(-dx, -dy), make(n, dx, dy)) for n, (dx, dy) in enumerate(NEAR)]

    def rc(src, dst, ss, rs, dev):
        return pltpu.make_async_remote_copy(
            src_ref=src, dst_ref=dst, send_sem=ss, recv_sem=rs, device_id=dev, device_id_type=MESH
        )

    def dev_near(dx, dy):
        return {"gx": gx + dx, "gy": gy + dy}

    c0 = near_copies(lambda n, dx, dy: rc(
        E0.at[:, sl(SRC0X[dx]), sl(SRC0Y[dy])], E0.at[:, sl(DST0X[dx]), sl(DST0Y[dy])], e0s.at[n], e0r.at[n], dev_near(dx, dy)))
    c1 = near_copies(lambda n, dx, dy: rc(
        E1.at[sl(SRC1X[dx]), sl(SRC1Y[dy])], E1.at[sl(DST1X[dx]), sl(DST1Y[dy])], e1s.at[n], e1r.at[n], dev_near(dx, dy)))
    cx = near_copies(lambda n, dx, dy: rc(
        XB.at[1, :, :, sl(SRC0Y[dy])], XB.at[1 - dx, :, :, sl(DST0Y[dy])], xs.at[n], xr.at[n], dev_near(dx, dy)))

    def close(a, b, sign):
        px, py = rem(gx + sign * a + 4, 4), rem(gy + sign * b + 8, 8)
        return (jnp.abs(px - gx) <= 2) & (jnp.abs(py - gy) <= 1)

    gather, gather_z = [], []
    for n, (a, b) in enumerate(PLANE):
        px, py = peer(a, b)
        dev = {"gx": px, "gy": py}
        wide = rc(E23.at[own, 0:3], E23.at[own, 0:3], gs.at[n], gr.at[n], dev)
        thin = rc(E23.at[own, 2:3], E23.at[own, 2:3], gs.at[n], gr.at[n], dev)
        gather.append((wide, thin, close(a, b, 1), close(a, b, -1)))
        gather_z.append(rc(E23.at[own, 3:5], E23.at[own, 3:5], cs.at[n], cr.at[n], dev))

    for ok, _, c in c0:
        each(ok, [c], "start")
    for ok, _, c in c1:
        each(ok, [c], "start")
    for wide, thin, near, _ in gather:
        each(near, [wide], "start")
        each(jnp.logical_not(near), [thin], "start")

    @pl.when(gz == 0)
    def _():
        for n in range(3):
            XB[1, 0, n, 8:40] = zero32
        E23[own, 3] = zero8

    @pl.when(gz == 7)
    def _():
        for n in range(3):
            XB[1, 1, n, 8:40] = zero32
        E23[own, 4] = zero8

    each(gz < 7, [zdown[3]], "wait_recv")
    each(gz > 0, [zup[3]], "wait_recv")
    for c in gather_z:
        c.start()
    each(gz < 7, zdown[0:3], "wait_recv")
    each(gz > 0, zup[0:3], "wait_recv")
    for ok, _, c in cx:
        each(ok, [c], "start")

    for _, okr, c in c0:
        each(okr, [c], "wait_recv")

    def load0(i):
        m = mask0(i)
        L0.K[i, 8:56] = jnp.where(m, E0[1, i], 0.0)
        L0.R[i] = jnp.where(m, E0[0, i], 0.0)

    loop(0, 30, load0)
    L0.build()
    L0.smooth6()

    for wide, thin, _, near in gather:
        each(near, [wide], "wait_recv")
        each(jnp.logical_not(near), [thin], "wait_recv")
    for c in gather_z:
        c.wait_recv()
    top = rowid(8) < 4
    in3 = yz(8, 0, 8, 16, 16, 16)
    for sx in range(4):
        def load3(q, sx=sx):
            sa, sb = sx * 8 + 2 * q, sx * 8 + 2 * q + 1
            m = jnp.where(top, E23[sa, 2], E23[sb, 2])
            lo = jnp.where(top, E23[sa, 3], E23[sb, 3])
            hi = jnp.where(top, E23[sa, 4], E23[sb, 4])
            row = pl.multiple_of(8 * q, 8)
            for xl in range(2):
                for isk in range(2):
                    at = 32 * xl + 16 * isk
                    out = jnp.where(
                        l8 < 16, roll(m, (128 - at) % 128),
                        jnp.where(l8 < 32, roll(hi, (16 - 64 - at) % 128), roll(lo, (112 - 64 - at) % 128)),
                    )
                    out = jnp.where(in3, out, 0.0)
                    if isk:
                        L3.K[1 + 2 * sx + xl, pl.ds(8 + row, 8)] = out
                    else:
                        L3.R[1 + 2 * sx + xl, pl.ds(row, 8)] = out

        loop(0, 4, load3)
    L3.build()
    L3.step(L3.VA, L3.VB, A1, B1, 0, True)

    def residue(i):
        _, av = L3.flux(L3.VB, i)
        RES[i - 1] = L3.R[i] - av

    loop(1, 9, residue)
    in4 = mask4(0)

    def down4(x):
        t = (RES[2 * x, pl.ds(0, 16, stride=2)] + RES[2 * x, pl.ds(1, 16, stride=2)]) + (
            RES[2 * x + 1, pl.ds(0, 16, stride=2)] + RES[2 * x + 1, pl.ds(1, 16, stride=2)]
        )
        L4.R[1 + x] = jnp.where(in4, pair(t, 16), 0.0)
        t = (L3.K[1 + 2 * x, pl.ds(8, 16, stride=2)] + L3.K[1 + 2 * x, pl.ds(9, 16, stride=2)]) + (
            L3.K[2 + 2 * x, pl.ds(8, 16, stride=2)] + L3.K[2 + 2 * x, pl.ds(9, 16, stride=2)]
        )
        L4.K[1 + x, 8:24] = jnp.where(in4, 0.125 * pair(t, 16), 0.0)

    loop(0, 4, down4)
    L4.build()
    L4.step(L4.VA, L4.VB, A1, B1, 0, True)
    L4.step(L4.VB, L4.VA, A2, B2, 0)
    L4.step(L4.VA, L4.VB, A3, B3, 0)

    def repeat_lanes(x, rows):
        l = lanes(rows)
        return gat(x, jnp.where(l < 96, l >> 1, (l >> 1) + 64))

    def repeat_rows(ref, x, rows):
        ref[pl.ds(0, rows, stride=2)] = x
        ref[pl.ds(1, rows, stride=2)] = x

    def up4(x):
        repeat_rows(T, repeat_lanes(L4.VB[1 + x, 8:24], 16), 16)
        for p in range(2):
            L3.VB[1 + 2 * x + p, 8:40] = L3.VB[1 + 2 * x + p, 8:40] + T[0:32]

    loop(0, 4, up4)
    L3.step(L3.VB, L3.VA, 0.0, B0, 0)
    L3.step(L3.VA, L3.VB, A1, B1, 0)

    def load2(i):
        xg = 4 * gx + i - 7 + 8
        sx = (xg >> 2) - 2
        xl = xg & 3
        scx = jnp.clip(sx, 0, 3)
        m = mask2(i)
        for n in range(3):
            sy = jnp.clip(gy + n - 1, 0, 7)
            slot = scx * 8 + sy
            r, k, lo, hi = E23[slot, 0], E23[slot, 1], E23[slot, 3], E23[slot, 4]
            mn = m[8 * n : 8 * n + 8]
            for isk, mid in ((0, r), (1, k)):
                at = 8 * xl + 32 * isk
                out = jnp.where(
                    l8 < 32, roll(mid, (128 - 32 * xl) & 127),
                    jnp.where(l8 < 64, roll(hi, (160 - at) & 127), roll(lo, (248 - at) & 127)),
                )
                out = jnp.where(mn, out, 0.0)
                if isk:
                    L2.K[i, 8 + 8 * n : 16 + 8 * n] = out
                else:
                    L2.R[i, 8 * n : 8 * n + 8] = out

    loop(0, 18, load2)
    L2.build()
    L2.smooth6()

    def up3(q):
        w = L3.VB[2 * gx + q, pl.ds(4 * gy + 4, 16)]
        repeat_rows(T, repeat_lanes(w, 16), 16)
        for p in range(2):
            L2.VB[2 * q + 5 + p, 8:32] = L2.VB[2 * q + 5 + p, 8:32] + T[0:24]

    loop(0, 4, up3)

    for _, okr, c in c1:
        each(okr, [c], "wait_recv")
    for _, okr, c in cx:
        each(okr, [c], "wait_recv")

    l32b = lanes(32)

    def load1(i):
        x = i - 7
        dx = jnp.where(x >= 0, 1, 0) + jnp.where(x >= 8, 1, 0)
        xl = x & 7
        m = mask1(i)
        main = E1[i]
        lo = jnp.concatenate([XB[dx, 0, 2, 0:16], XB[dx, 0, 2, 32:48]], axis=0)
        hi = jnp.concatenate([XB[dx, 1, 2, 0:16], XB[dx, 1, 2, 32:48]], axis=0)
        for isk in range(2):
            at = 8 * xl + 64 * isk
            mid = roll(main, 64) if isk else main
            out = jnp.where(
                l32b < 64, mid,
                jnp.where(l32b < 96, roll(hi, (192 - at) & 127), roll(lo, (248 - at) & 127)),
            )
            out = jnp.where(m, out, 0.0)
            if isk:
                L1.K[i, 8:40] = out
            else:
                L1.R[i] = out

    loop(0, 22, load1)
    L1.build()
    L1.smooth6()

    def up2(q):
        repeat_rows(T, repeat_lanes(L2.VB[q + 6, 12:28], 16), 16)
        for p in range(2):
            L1.VB[2 * q + 5 + p, 8:40] = L1.VB[2 * q + 5 + p, 8:40] + T[0:32]

    loop(0, 6, up2)

    ls, gsl, zz = group(48)

    def load_slab(xi):
        m = masks(xi + 1)
        x = 10 * gsl + (xi - 7)
        which = jnp.where(x >= 0, 1, 0) + jnp.where(x >= 16, 1, 0)
        xl = x & 15
        ilo = (8 * xl + zz) & 127
        ihi = (8 * xl + zz - 34) & 127
        imain = jnp.where(zz < 21, zz - 8, zz + 94) & 127
        for arr in range(2):
            src = L0.K if arr else L0.R
            parts = []
            for g in range(3):
                plane = src[10 * g + xi, 8:56] if arr else src[10 * g + xi]
                parts.append(gat(plane, imain))
            mid = jnp.where(gsl == 0, parts[0], jnp.where(gsl == 1, parts[1], parts[2]))
            lo = [gat(XB[d, 0, arr], ilo) for d in range(3)]
            hi = [gat(XB[d, 1, arr], ihi) for d in range(3)]
            pick = [jnp.where(which == 0, t[0], jnp.where(which == 1, t[1], t[2])) for t in (lo, hi)]
            out = jnp.where(zz < 8, pick[0], jnp.where(zz >= 34, pick[1], mid))
            out = jnp.where(m, out, 0.0)
            if arr:
                LS.K[1 + xi, 8:56] = out
            else:
                LS.R[1 + xi] = out

    loop(0, 10, load_slab)

    def ghosts(ref):
        ref[0, 8:56] = roll(ref[10, 8:56], 42)
        ref[11, 8:56] = roll(ref[1, 8:56], 86)

    ghosts(LS.K)
    LS.build()
    ghosts(LS.VA)
    LS.smooth6(after=ghosts, trim=False)

    l48, l24 = lanes(48), lanes(24)

    def merge(q):
        w = L1.VB[q + 6, 12:36]
        repeat_rows(T, gat(w, l24 >> 1), 24)
        repeat_rows(TH, gat(w, jnp.where(l24 == 0, 127, 64)), 24)
        for p in range(2):
            i = 2 * q + 5 + p
            g = jnp.where(i >= 10, 1, 0) + jnp.where(i >= 20, 1, 0)
            xi = i - 10 * g
            sv = LS.VB[1 + xi, 8:56]
            sk = LS.K[1 + xi, 8:56]
            off = 42 * g
            v = jnp.where(
                l48 < 6, roll(sv, (248 - off) & 127),
                jnp.where(l48 >= 122, roll(sv, (222 - off) & 127), L0.VB[i, 8:56]),
            )
            L0.VB[i, 8:56] = v + T[0:48]
            HV[i] = jnp.where(l48 < 64, roll(sv, (249 - off) & 127), roll(sv, (221 - off) & 127)) + TH[0:48]
            KH[i] = jnp.where(l48 < 64, roll(sk, (249 - off) & 127), roll(sk, (221 - off) & 127))

    loop(0, 10, merge)

    def final(x):
        i = x + 7
        c = slice(16, 48)
        v = L0.VB[i, c]
        k = L0.K[i, c]
        hv, kh = HV[i, 8:40], KH[i, 8:40]
        out = L0.CX[i, 8:40] * (v - L0.VB[i - 1, c])
        out = out + L0.CX[i + 1, 8:40] * (v - L0.VB[i + 1, c])
        out = out + L0.CY[i, 8:40] * (v - L0.VB[i, 15:47])
        out = out + L0.CY[i, 9:41] * (v - L0.VB[i, 17:49])
        cl = 0.5 * (k + jnp.where(l32 == 0, kh, roll(k, 1)))
        cr = 0.5 * (k + jnp.where(l32 == 127, kh, roll(k, 127)))
        out = out + cl * (v - jnp.where(l32 == 0, hv, roll(v, 1)))
        out = out + cr * (v - jnp.where(l32 == 127, hv, roll(v, 127)))
        corr_out[x] = v
        res_out[x] = r_in[x] - out

    loop(0, 16, final)

    each(gz > 0, zdown, "wait_send")
    each(gz < 7, zup, "wait_send")
    for ok, _, c in c0 + c1 + cx:
        each(ok, [c], "wait_send")
    for wide, thin, near, _ in gather:
        each(near, [wide], "wait_send")
        each(jnp.logical_not(near), [thin], "wait_send")
    for c in gather_z:
        c.wait_send()


def level_scratch(X, Y):
    big, mid = pltpu.VMEM((X, Y + 16, 128), f32), pltpu.VMEM((X, Y, 128), f32)
    return [big, mid, mid, pltpu.VMEM((X, Y + 8, 128), f32), mid, mid, big, big]


def shards(source, conductivity):
    dma = pltpu.SemaphoreType.DMA
    vm = lambda *shape: pltpu.VMEM(shape, f32)
    out = jax.ShapeDtypeStruct((16, 32, 128), f32)
    scratch = [
        vm(2, 30, 48, 128), vm(22, 32, 128), vm(32, 5, 8, 128), vm(3, 2, 3, 48, 128), vm(2, 3, 32, 128),
        vm(4, 8, 128), vm(48, 128), vm(48, 128), vm(8, 32, 128), vm(30, 48, 128), vm(30, 48, 128),
        dma((2,)), dma((8,)), dma((8,)), dma((8,)), dma((8,)), dma((31,)), dma((31,)), dma((2, 4)), dma((2, 4)),
        dma((8,)), dma((8,)), dma((31,)), dma((31,)),
    ]
    for X, Y in ((30, 48), (12, 48), (22, 32), (18, 24), (10, 32), (6, 16)):
        scratch += level_scratch(X, Y)
    return pl.pallas_call(
        kernel,
        out_shape=(out, out),
        in_specs=[pl.BlockSpec(memory_space=pltpu.VMEM)] * 2,
        out_specs=(pl.BlockSpec(memory_space=pltpu.VMEM),) * 2,
        scratch_shapes=scratch,
        compiler_params=pltpu.CompilerParams(
            collective_id=0, has_side_effects=True, vmem_limit_bytes=48 * 1024 * 1024
        ),
        name="multigrid",
    )(source, conductivity)


def solution(mesh):
    spec = P("gx", "gy", "gz")
    return jax.shard_map(shards, mesh=mesh, in_specs=(spec, spec), out_specs=(spec, spec), check_vma=False)
```

```python
import jax
import jax.numpy as jnp
from jax import lax
from jax.experimental import pallas as pl
from jax.experimental.pallas import tpu as pltpu
from jax.sharding import PartitionSpec as P

f32 = jnp.float32
MESH = pl.DeviceIdType.MESH

CENTRE = (2.0 + 0.3) / 2.0
HALF = (2.0 - 0.3) / 2.0
SHARP = CENTRE / HALF
W0 = 1.0 / SHARP
W1 = 1.0 / (2.0 * SHARP - W0)
W2 = 1.0 / (2.0 * SHARP - W1)
W3 = 1.0 / (2.0 * SHARP - W2)
B0 = 1.0 / CENTRE
A1, B1 = W1 * W0, 2.0 * W1 / HALF
A2, B2 = W2 * W1, 2.0 * W2 / HALF
A3, B3 = W3 * W2, 2.0 * W3 / HALF

NEAR = [(dx, dy) for dx in (-1, 0, 1) for dy in (-1, 0, 1) if (dx, dy) != (0, 0)]
PLANE = [(a, b) for a in range(4) for b in range(8) if (a, b) != (0, 0)]


def lanes(rows):
    return lax.broadcasted_iota(jnp.int32, (rows, 128), 1)


def rowid(rows):
    return lax.broadcasted_iota(jnp.int32, (rows, 128), 0)


def gat(x, idx):
    return jnp.take_along_axis(x, idx, axis=1, mode="promise_in_bounds")


def roll(x, shift):
    return pltpu.roll(x, shift, 1)


def loop(lo, hi, width, body):
    def chunk(first, count):
        stores = [st for u in range(count) for st in body(first + u)]
        for ref, index, value in stores:
            ref[index] = value

    def step(j, c):
        chunk(lo + j * width, width)
        return c

    whole = (hi - lo) // width
    if whole == 1:
        chunk(lo, width)
    elif whole > 1:
        lax.fori_loop(0, whole, step, 0)
    if (hi - lo) % width:
        chunk(lo + whole * width, (hi - lo) % width)


def rem(a, n):
    return lax.rem(a, n)


class Level:
    def __init__(self, refs, planes, rows, factor, mask, width):
        self.K, self.R, self.CX, self.CY, self.CZ, self.CW, self.ID, self.VA, self.VB = refs
        self.width = width
        self.X, self.Y, self.h, self.mask = planes, rows, 0.5 * factor, mask

    def clear(self):
        Y = self.Y
        pad = jnp.zeros((8, 128), f32)

        def body(i):
            out = []
            for ref in (self.K, self.VA, self.VB):
                out += [(ref, (i, slice(0, 8)), pad), (ref, (i, slice(8 + Y, 16 + Y)), pad)]
            return out

        loop(0, self.X, 6, body)
        full = jnp.zeros((Y, 128), f32)
        for i in (0, self.X - 1):
            for ref in (self.VA, self.VB, self.K):
                ref[i, 8 : 8 + Y] = full

    def build(self):
        Y, h, K = self.Y, self.h, self.K

        def body(i):
            k = K[i, 8 : 8 + Y]
            low = h * (k + K[i - 1, 8 : 8 + Y])
            high = h * (k + K[i + 1, 8 : 8 + Y])
            cy = h * (K[i, 8 : 16 + Y] + K[i, 7 : 15 + Y])
            cz = h * (k + roll(k, 1))
            cw = h * (k + roll(k, 127))
            ylow = h * (k + K[i, 7 : 7 + Y])
            yhigh = h * (k + K[i, 9 : 9 + Y])
            d = low + high + ylow + yhigh + cz + cw
            inv = jnp.where(self.mask(i), 1.0 / d, 0.0)
            first = B0 * (self.R[i] * inv)
            return [
                (self.CX, i, low), (self.CX, i + 1, high), (self.CY, i, cy), (self.CZ, i, cz), (self.CW, i, cw),
                (self.ID, i, inv), (self.VA, (i, slice(8, 8 + Y)), first),
            ]

        loop(1, self.X - 1, self.width, body)

    def flux(self, V, i):
        Y = self.Y
        v = V[i, 8 : 8 + Y]
        out = self.CX[i] * (v - V[i - 1, 8 : 8 + Y])
        out = out + self.CX[i + 1] * (v - V[i + 1, 8 : 8 + Y])
        out = out + self.CY[i, 0:Y] * (v - V[i, 7 : 7 + Y])
        out = out + self.CY[i, 1 : 1 + Y] * (v - V[i, 9 : 9 + Y])
        out = out + self.CZ[i] * (v - roll(v, 1))
        return v, out + self.CW[i] * (v - roll(v, 127))

    def step(self, src, dst, a, b, shrink, first=False):
        Y = self.Y

        def body(i):
            v, av = self.flux(src, i)
            new = v + b * (self.ID[i] * (self.R[i] - av))
            if first:
                new = new + a * v
            elif a != 0.0:
                new = new + a * (v - dst[i, 8 : 8 + Y])
            return [(dst, (i, slice(8, 8 + Y)), new)]

        loop(1 + shrink, self.X - 1 - shrink, self.width, body)

    def smooth6(self, after=None, trim=True):
        plan = [
            (self.VA, self.VB, A1, B1, True),
            (self.VB, self.VA, A2, B2, False),
            (self.VA, self.VB, 0.0, B0, False),
            (self.VB, self.VA, A1, B1, False),
            (self.VA, self.VB, A2, B2, False),
        ]
        for n, (src, dst, a, b, first) in enumerate(plan):
            self.step(src, dst, a, b, n + 1 if trim else 0, first)
            if after is not None and n < 4:
                after(dst)


def kernel(r_in, k_in, corr_out, res_out, *s):
    (E0, E1, E23, XB, PB, RK2, T, TH, RES, HV, KH, sem_loc, e0s, e0r, e1s, e1r, gs, gr, bs, br, xs, xr, cs, cr, *lv) = s
    gx, gy, gz = lax.axis_index("gx"), lax.axis_index("gy"), lax.axis_index("gz")
    own = gx * 8 + gy

    bar = pltpu.get_barrier_semaphore()

    def peer(a, b):
        return rem(gx + a, 4), rem(gy + b, 8)

    for a, b in PLANE:
        px, py = peer(a, b)
        pl.semaphore_signal(bar, inc=1, device_id={"gx": px, "gy": py}, device_id_type=MESH)

    @pl.when(gz > 0)
    def _():
        pl.semaphore_signal(bar, inc=1, device_id={"gz": gz - 1}, device_id_type=MESH)

    @pl.when(gz < 7)
    def _():
        pl.semaphore_signal(bar, inc=1, device_id={"gz": gz + 1}, device_id_type=MESH)

    def yz(rows, ylo, ny, zlo, zown, zhi):
        y = rowid(rows) + ylo
        l = lanes(rows)
        low = jnp.where(gz > 0, 128 - zlo, 128)
        high = jnp.where(gz < 7, zown + zhi, zown)
        return (y >= 0) & (y < ny) & ((l < high) | (l >= low))

    def with_x(base, rows, x, nx):
        xv = jnp.zeros((rows, 128), jnp.int32) + x
        return base & (xv >= 0) & (xv < nx)

    def mask0(i):
        return with_x(yz(48, 32 * gy - 8, 256, 0, 128, 0), 48, 16 * gx + i - 7, 64)

    def group(rows):
        l = lanes(rows)
        g = jnp.where(l >= 84, 2, jnp.where(l >= 42, 1, 0))
        return l, g, l - 42 * g

    def masks(i):
        l, g, zz = group(48)
        y = rowid(48) + (32 * gy - 8)
        x = 10 * g + (16 * gx + i - 8)
        low = jnp.where(gz > 0, 0, 8)
        high = jnp.where(gz < 7, 42, 34)
        return (y >= 0) & (y < 256) & (x >= 0) & (x < 64) & (zz >= low) & (zz < high) & (l < 126)

    def mask1(i):
        return with_x(yz(32, 16 * gy - 8, 128, 8, 64, 8), 32, 8 * gx + i - 7, 32)

    def mask2(i):
        return with_x(yz(24, 8 * gy - 8, 64, 8, 32, 8), 24, 4 * gx + i - 7, 16)

    def mask3(i):
        return yz(32, 0, 32, 16, 16, 16)

    def mask4(i):
        return yz(16, 0, 16, 8, 8, 8)

    L0 = Level(lv[0:9], 30, 48, 1.0, mask0, 2)
    LS = Level(lv[9:18], 12, 48, 1.0, masks, 2)
    L1 = Level(lv[18:27], 22, 32, 2.0, mask1, 3)
    L2 = Level(lv[27:36], 18, 24, 4.0, mask2, 4)
    L3 = Level(lv[36:45], 10, 32, 8.0, mask3, 4)
    L4 = Level(lv[45:54], 6, 16, 16.0, mask4, 4)

    loc = [
        pltpu.make_async_copy(ref, E0.at[n, 7:23, 8:40], sem_loc.at[n]) for n, ref in enumerate((r_in, k_in))
    ]
    for c in loc:
        c.start()

    l32 = lanes(32)
    zero32 = jnp.zeros((32, 128), f32)

    def pack0(x, c):
        r8, k8 = roll(r_in[x], 8 * x), roll(k_in[x], 8 * x)
        here, before = (l32 >> 3) == x, (l32 >> 3) == ((x + 15) & 15)
        return (
            jnp.where(here, r8, c[0]),
            jnp.where(here, k8, c[1]),
            jnp.where(before, r8, c[2]),
            jnp.where(before, k8, c[3]),
        )

    packed = (zero32,) * 4
    for x in range(16):
        packed = pack0(x, packed)
    PB[0, 0], PB[0, 1] = packed[0], packed[1]
    PB[1, 0], PB[1, 1] = roll(packed[2], 8), roll(packed[3], 8)

    def pair(x, rows):
        l = lanes(rows)
        return gat(x, (2 * l) & 127) + gat(x, (2 * l + 1) & 127)

    l16 = lanes(16)

    def down1(x, c):
        out = []
        for ref in (r_in, k_in):
            t = (ref[2 * x, pl.ds(0, 16, stride=2)] + ref[2 * x, pl.ds(1, 16, stride=2)]) + (
                ref[2 * x + 1, pl.ds(0, 16, stride=2)] + ref[2 * x + 1, pl.ds(1, 16, stride=2)]
            )
            out.append(pair(t, 16))
        rk = jnp.where(l16 < 64, out[0], 0.125 * out[1])
        E1[7 + x, 8:24] = rk
        here = ((l16 & 63) >> 3) == x
        return (
            jnp.where(here, roll(rk, 8 * x), c[0]),
            jnp.where(here, roll(rk, (8 * x + 72) & 127), c[1]),
        )

    zero16 = jnp.zeros((16, 128), f32)
    low1 = high1 = zero16
    for x in range(8):
        low1, high1 = down1(x, (low1, high1))
    for side, val in enumerate((low1, high1)):
        PB[side, 2, 0:8] = val[0:8]
        PB[side, 2, 24:32] = val[8:16]

    l8 = lanes(8)
    zero8 = jnp.zeros((8, 128), f32)

    def down2(x, c):
        def part(p, n):
            return E1[7 + 2 * x + p, pl.ds(8 + n, 8, stride=2)]

        t = (part(0, 0) + part(0, 1)) + (part(1, 0) + part(1, 1))
        rk = pair(t, 8)
        rk = jnp.where(((l8 >> 5) & 1) == 1, 0.125 * rk, rk)
        RK2[x] = rk
        here, edge = (l8 >> 5) == x, (l8 < 64) & (((l8 & 31) >> 3) == x)
        return (
            jnp.where(here, roll(rk, 32 * x), c[0]),
            jnp.where(here, roll(rk, (32 * x + 96) & 127), c[1]),
            jnp.where(edge, roll(rk, 8 * x), c[2]),
            jnp.where(edge, roll(rk, (8 * x + 104) & 127), c[3]),
        )

    r2 = k2 = low2 = high2 = zero8
    for x in range(4):
        r2, k2, low2, high2 = down2(x, (r2, k2, low2, high2))
    l4 = lanes(4)
    rk3 = []
    for x in range(2):
        t = (RK2[2 * x, pl.ds(0, 4, stride=2)] + RK2[2 * x, pl.ds(1, 4, stride=2)]) + (
            RK2[2 * x + 1, pl.ds(0, 4, stride=2)] + RK2[2 * x + 1, pl.ds(1, 4, stride=2)]
        )
        T[x, 0:4], T[x, 4:8] = t, t
        t = pair(T[x, 0:8], 8)
        rk3.append(jnp.where(((l8 >> 4) & 1) == 1, 0.125 * t, t))
    m3 = jnp.where(((l8 >> 5) & 1) == 0, rk3[0], rk3[1])
    E23[own, 0], E23[own, 1], E23[own, 2] = r2, k2, m3
    RK2[0] = jnp.where(l8 < 64, low2, m3)
    RK2[1] = jnp.where(l8 < 64, high2, m3)

    for L in (L0, LS, L1, L2, L3, L4):
        L.clear()

    pl.semaphore_wait(bar, 31 + jnp.where(gz > 0, 1, 0) + jnp.where(gz < 7, 1, 0))

    def zcopies(side):
        dev = {"gz": gz - 1 if side == 0 else gz + 1}
        land = 1 - side
        pieces = [
            (PB.at[side, 0:2], XB.at[1, land, 0:2, 8:40]),
            (PB.at[side, 2, 0:8], XB.at[1, land, 2, 8:16]),
            (PB.at[side, 2, 24:32], XB.at[1, land, 2, 32:40]),
            (RK2.at[side], E23.at[own, 3 + land]),
        ]
        return [
            pltpu.make_async_remote_copy(
                src_ref=src, dst_ref=dst, send_sem=bs.at[side, n], recv_sem=br.at[side, n],
                device_id=dev, device_id_type=MESH,
            )
            for n, (src, dst) in enumerate(pieces)
        ]

    def each(cond, copies, what):
        @pl.when(cond)
        def _():
            for c in copies:
                getattr(c, what)()

    zdown, zup = zcopies(0), zcopies(1)
    each(gz > 0, zdown[::-1], "start")
    each(gz < 7, zup[::-1], "start")

    for c in loc:
        c.wait()

    def inside(dx, dy):
        return (gx + dx >= 0) & (gx + dx < 4) & (gy + dy >= 0) & (gy + dy < 8)

    SRC0X, DST0X = {-1: (7, 14), 0: (7, 23), 1: (16, 23)}, {-1: (23, 30), 0: (7, 23), 1: (0, 7)}
    SRC0Y, DST0Y = {-1: (8, 16), 0: (8, 40), 1: (32, 40)}, {-1: (40, 48), 0: (8, 40), 1: (0, 8)}
    SRC1X, DST1X = {-1: (7, 14), 0: (7, 15), 1: (8, 15)}, {-1: (15, 22), 0: (7, 15), 1: (0, 7)}
    SRC1Y, DST1Y = {-1: (8, 16), 0: (8, 24), 1: (16, 24)}, {-1: (24, 32), 0: (8, 24), 1: (0, 8)}

    def sl(pairs):
        return pl.ds(pairs[0], pairs[1] - pairs[0])

    def near_copies(make):
        return [(inside(dx, dy), inside(-dx, -dy), make(n, dx, dy)) for n, (dx, dy) in enumerate(NEAR)]

    def rc(src, dst, ss, rs, dev):
        return pltpu.make_async_remote_copy(
            src_ref=src, dst_ref=dst, send_sem=ss, recv_sem=rs, device_id=dev, device_id_type=MESH
        )

    def dev_near(dx, dy):
        return {"gx": gx + dx, "gy": gy + dy}

    c0 = near_copies(lambda n, dx, dy: rc(
        E0.at[:, sl(SRC0X[dx]), sl(SRC0Y[dy])], E0.at[:, sl(DST0X[dx]), sl(DST0Y[dy])], e0s.at[n], e0r.at[n], dev_near(dx, dy)))
    c1 = near_copies(lambda n, dx, dy: rc(
        E1.at[sl(SRC1X[dx]), sl(SRC1Y[dy])], E1.at[sl(DST1X[dx]), sl(DST1Y[dy])], e1s.at[n], e1r.at[n], dev_near(dx, dy)))
    cx = near_copies(lambda n, dx, dy: rc(
        XB.at[1, :, :, sl(SRC0Y[dy])], XB.at[1 - dx, :, :, sl(DST0Y[dy])], xs.at[n], xr.at[n], dev_near(dx, dy)))

    def close(a, b, sign):
        px, py = rem(gx + sign * a + 4, 4), rem(gy + sign * b + 8, 8)
        return (jnp.abs(px - gx) <= 2) & (jnp.abs(py - gy) <= 1)

    gather, gather_z = [], []
    for n, (a, b) in enumerate(PLANE):
        px, py = peer(a, b)
        dev = {"gx": px, "gy": py}
        wide = rc(E23.at[own, 0:3], E23.at[own, 0:3], gs.at[n], gr.at[n], dev)
        thin = rc(E23.at[own, 2:3], E23.at[own, 2:3], gs.at[n], gr.at[n], dev)
        gather.append((wide, thin, close(a, b, 1), close(a, b, -1)))
        gather_z.append(rc(E23.at[own, 3:5], E23.at[own, 3:5], cs.at[n], cr.at[n], dev))

    for ok, _, c in c0:
        each(ok, [c], "start")
    for ok, _, c in c1:
        each(ok, [c], "start")
    for wide, thin, near, _ in gather:
        each(near, [wide], "start")
        each(jnp.logical_not(near), [thin], "start")

    @pl.when(gz == 0)
    def _():
        for n in range(3):
            XB[1, 0, n, 8:40] = zero32
        E23[own, 3] = zero8

    @pl.when(gz == 7)
    def _():
        for n in range(3):
            XB[1, 1, n, 8:40] = zero32
        E23[own, 4] = zero8

    each(gz < 7, [zdown[3]], "wait_recv")
    each(gz > 0, [zup[3]], "wait_recv")
    for c in gather_z:
        c.start()
    each(gz < 7, zdown[0:3], "wait_recv")
    each(gz > 0, zup[0:3], "wait_recv")
    for ok, _, c in cx:
        each(ok, [c], "start")

    for _, okr, c in c0:
        each(okr, [c], "wait_recv")

    def load0(i):
        m = mask0(i)
        return [
            (L0.K, (i, slice(8, 56)), jnp.where(m, E0[1, i], 0.0)), (L0.R, i, jnp.where(m, E0[0, i], 0.0)),
        ]

    loop(0, 30, 3, load0)
    L0.build()
    L0.smooth6()

    for wide, thin, _, near in gather:
        each(near, [wide], "wait_recv")
        each(jnp.logical_not(near), [thin], "wait_recv")
    for c in gather_z:
        c.wait_recv()
    top = rowid(8) < 4
    in3 = yz(8, 0, 8, 16, 16, 16)
    for sx in range(4):
        def load3(q, sx=sx):
            sa, sb = sx * 8 + 2 * q, sx * 8 + 2 * q + 1
            m = jnp.where(top, E23[sa, 2], E23[sb, 2])
            lo = jnp.where(top, E23[sa, 3], E23[sb, 3])
            hi = jnp.where(top, E23[sa, 4], E23[sb, 4])
            out3 = []
            for xl in range(2):
                for isk in range(2):
                    at = 32 * xl + 16 * isk
                    out = jnp.where(
                        l8 < 16, roll(m, (128 - at) % 128),
                        jnp.where(l8 < 32, roll(hi, (16 - 64 - at) % 128), roll(lo, (112 - 64 - at) % 128)),
                    )
                    out = jnp.where(in3, out, 0.0)
                    plane = 1 + 2 * sx + xl
                    if isk:
                        out3.append((L3.K, (plane, slice(8 + 8 * q, 16 + 8 * q)), out))
                    else:
                        out3.append((L3.R, (plane, slice(8 * q, 8 * q + 8)), out))
            return out3

        loop(0, 4, 4, load3)
    L3.build()
    L3.step(L3.VA, L3.VB, A1, B1, 0, True)

    def residue(i):
        _, av = L3.flux(L3.VB, i)
        return [(RES, i - 1, L3.R[i] - av)]

    loop(1, 9, 4, residue)
    in4 = mask4(0)

    def down4(x):
        t = (RES[2 * x, pl.ds(0, 16, stride=2)] + RES[2 * x, pl.ds(1, 16, stride=2)]) + (
            RES[2 * x + 1, pl.ds(0, 16, stride=2)] + RES[2 * x + 1, pl.ds(1, 16, stride=2)]
        )
        r4 = jnp.where(in4, pair(t, 16), 0.0)
        t = (L3.K[1 + 2 * x, pl.ds(8, 16, stride=2)] + L3.K[1 + 2 * x, pl.ds(9, 16, stride=2)]) + (
            L3.K[2 + 2 * x, pl.ds(8, 16, stride=2)] + L3.K[2 + 2 * x, pl.ds(9, 16, stride=2)]
        )
        k4 = jnp.where(in4, 0.125 * pair(t, 16), 0.0)
        return [(L4.R, 1 + x, r4), (L4.K, (1 + x, slice(8, 24)), k4)]

    loop(0, 4, 4, down4)
    L4.build()
    L4.step(L4.VA, L4.VB, A1, B1, 0, True)
    L4.step(L4.VB, L4.VA, A2, B2, 0)
    L4.step(L4.VA, L4.VB, A3, B3, 0)

    def repeat_lanes(x, rows):
        l = lanes(rows)
        return gat(x, jnp.where(l < 96, l >> 1, (l >> 1) + 64))

    def repeat_rows(ref, slot, x, rows):
        ref[slot, pl.ds(0, rows, stride=2)] = x
        ref[slot, pl.ds(1, rows, stride=2)] = x
        return ref[slot, 0 : 2 * rows]

    def up4(x):
        t = repeat_rows(T, x, repeat_lanes(L4.VB[1 + x, 8:24], 16), 16)
        rows = slice(8, 40)
        return [(L3.VB, (1 + 2 * x + p, rows), L3.VB[1 + 2 * x + p, rows] + t) for p in range(2)]

    loop(0, 4, 4, up4)
    L3.step(L3.VB, L3.VA, 0.0, B0, 0)
    L3.step(L3.VA, L3.VB, A1, B1, 0)

    def load2(i):
        xg = 4 * gx + i - 7 + 8
        sx = (xg >> 2) - 2
        xl = xg & 3
        scx = jnp.clip(sx, 0, 3)
        m = mask2(i)
        out2 = []
        for n in range(3):
            sy = jnp.clip(gy + n - 1, 0, 7)
            slot = scx * 8 + sy
            r, k, lo, hi = E23[slot, 0], E23[slot, 1], E23[slot, 3], E23[slot, 4]
            mn = m[8 * n : 8 * n + 8]
            for isk, mid in ((0, r), (1, k)):
                at = 8 * xl + 32 * isk
                out = jnp.where(
                    l8 < 32, roll(mid, (128 - 32 * xl) & 127),
                    jnp.where(l8 < 64, roll(hi, (160 - at) & 127), roll(lo, (248 - at) & 127)),
                )
                out = jnp.where(mn, out, 0.0)
                if isk:
                    out2.append((L2.K, (i, slice(8 + 8 * n, 16 + 8 * n)), out))
                else:
                    out2.append((L2.R, (i, slice(8 * n, 8 * n + 8)), out))
        return out2

    loop(0, 18, 3, load2)
    L2.build()
    L2.smooth6()

    def up3(q):
        w = L3.VB[2 * gx + q, pl.ds(4 * gy + 4, 16)]
        t = repeat_rows(T, 4 + q, repeat_lanes(w, 16), 16)[0:24]
        rows = slice(8, 32)
        return [(L2.VB, (2 * q + 5 + p, rows), L2.VB[2 * q + 5 + p, rows] + t) for p in range(2)]

    loop(0, 4, 4, up3)

    for _, okr, c in c1:
        each(okr, [c], "wait_recv")
    for _, okr, c in cx:
        each(okr, [c], "wait_recv")

    l32b = lanes(32)

    def load1(i):
        x = i - 7
        dx = jnp.where(x >= 0, 1, 0) + jnp.where(x >= 8, 1, 0)
        xl = x & 7
        m = mask1(i)
        main = E1[i]
        out1 = []
        lo = jnp.concatenate([XB[dx, 0, 2, 0:16], XB[dx, 0, 2, 32:48]], axis=0)
        hi = jnp.concatenate([XB[dx, 1, 2, 0:16], XB[dx, 1, 2, 32:48]], axis=0)
        for isk in range(2):
            at = 8 * xl + 64 * isk
            mid = roll(main, 64) if isk else main
            out = jnp.where(
                l32b < 64, mid,
                jnp.where(l32b < 96, roll(hi, (192 - at) & 127), roll(lo, (248 - at) & 127)),
            )
            out = jnp.where(m, out, 0.0)
            if isk:
                out1.append((L1.K, (i, slice(8, 40)), out))
            else:
                out1.append((L1.R, i, out))
        return out1

    loop(0, 22, 2, load1)
    L1.build()
    L1.smooth6()

    def up2(q):
        t = repeat_rows(T, 8 + q, repeat_lanes(L2.VB[q + 6, 12:28], 16), 16)
        rows = slice(8, 40)
        return [(L1.VB, (2 * q + 5 + p, rows), L1.VB[2 * q + 5 + p, rows] + t) for p in range(2)]

    loop(0, 6, 6, up2)

    ls, gsl, zz = group(48)

    def load_slab(xi):
        m = masks(xi + 1)
        x = 10 * gsl + (xi - 7)
        which = jnp.where(x >= 0, 1, 0) + jnp.where(x >= 16, 1, 0)
        xl = x & 15
        ilo = (8 * xl + zz) & 127
        ihi = (8 * xl + zz - 34) & 127
        imain = jnp.where(zz < 21, zz - 8, zz + 94) & 127
        outs = []
        for arr in range(2):
            src = L0.K if arr else L0.R
            parts = []
            for g in range(3):
                plane = src[10 * g + xi, 8:56] if arr else src[10 * g + xi]
                parts.append(gat(plane, imain))
            mid = jnp.where(gsl == 0, parts[0], jnp.where(gsl == 1, parts[1], parts[2]))
            lo = [gat(XB[d, 0, arr], ilo) for d in range(3)]
            hi = [gat(XB[d, 1, arr], ihi) for d in range(3)]
            pick = [jnp.where(which == 0, t[0], jnp.where(which == 1, t[1], t[2])) for t in (lo, hi)]
            out = jnp.where(zz < 8, pick[0], jnp.where(zz >= 34, pick[1], mid))
            out = jnp.where(m, out, 0.0)
            if arr:
                outs.append((LS.K, (1 + xi, slice(8, 56)), out))
            else:
                outs.append((LS.R, 1 + xi, out))
        return outs

    loop(0, 10, 1, load_slab)

    def ghosts(ref):
        ref[0, 8:56] = roll(ref[10, 8:56], 42)
        ref[11, 8:56] = roll(ref[1, 8:56], 86)

    ghosts(LS.K)
    LS.build()
    ghosts(LS.VA)
    LS.smooth6(after=ghosts, trim=False)

    l48, l24 = lanes(48), lanes(24)

    def merge(q):
        w = L1.VB[q + 6, 12:36]
        t = repeat_rows(T, 14 + q, gat(w, l24 >> 1), 24)
        th = repeat_rows(TH, q, gat(w, jnp.where(l24 == 0, 127, 64)), 24)
        out = []
        for p in range(2):
            i = 2 * q + 5 + p
            g = jnp.where(i >= 10, 1, 0) + jnp.where(i >= 20, 1, 0)
            xi = i - 10 * g
            sv = LS.VB[1 + xi, 8:56]
            sk = LS.K[1 + xi, 8:56]
            off = 42 * g
            v = jnp.where(
                l48 < 6, roll(sv, (248 - off) & 127),
                jnp.where(l48 >= 122, roll(sv, (222 - off) & 127), L0.VB[i, 8:56]),
            )
            hv = jnp.where(l48 < 64, roll(sv, (249 - off) & 127), roll(sv, (221 - off) & 127)) + th
            kh = jnp.where(l48 < 64, roll(sk, (249 - off) & 127), roll(sk, (221 - off) & 127))
            out += [(L0.VB, (i, slice(8, 56)), v + t), (HV, i, hv), (KH, i, kh)]
        return out

    loop(0, 10, 1, merge)

    def final(x):
        i = x + 7
        c = slice(16, 48)
        v = L0.VB[i, c]
        k = L0.K[i, c]
        hv, kh = HV[i, 8:40], KH[i, 8:40]
        out = L0.CX[i, 8:40] * (v - L0.VB[i - 1, c])
        out = out + L0.CX[i + 1, 8:40] * (v - L0.VB[i + 1, c])
        out = out + L0.CY[i, 8:40] * (v - L0.VB[i, 15:47])
        out = out + L0.CY[i, 9:41] * (v - L0.VB[i, 17:49])
        cl = 0.5 * (k + jnp.where(l32 == 0, kh, roll(k, 1)))
        cr = 0.5 * (k + jnp.where(l32 == 127, kh, roll(k, 127)))
        out = out + cl * (v - jnp.where(l32 == 0, hv, roll(v, 1)))
        out = out + cr * (v - jnp.where(l32 == 127, hv, roll(v, 127)))
        return [(corr_out, x, v), (res_out, x, r_in[x] - out)]

    loop(0, 16, 2, final)

    each(gz > 0, zdown, "wait_send")
    each(gz < 7, zup, "wait_send")
    for ok, _, c in c0 + c1 + cx:
        each(ok, [c], "wait_send")
    for wide, thin, near, _ in gather:
        each(near, [wide], "wait_send")
        each(jnp.logical_not(near), [thin], "wait_send")
    for c in gather_z:
        c.wait_send()


def level_scratch(X, Y):
    big, mid = pltpu.VMEM((X, Y + 16, 128), f32), pltpu.VMEM((X, Y, 128), f32)
    return [big, mid, mid, pltpu.VMEM((X, Y + 8, 128), f32), mid, mid, mid, big, big]


def shards(source, conductivity):
    dma = pltpu.SemaphoreType.DMA
    vm = lambda *shape: pltpu.VMEM(shape, f32)
    out = jax.ShapeDtypeStruct((16, 32, 128), f32)
    scratch = [
        vm(2, 30, 48, 128), vm(22, 32, 128), vm(32, 5, 8, 128), vm(3, 2, 3, 48, 128), vm(2, 3, 32, 128),
        vm(4, 8, 128), vm(24, 48, 128), vm(10, 48, 128), vm(8, 32, 128), vm(30, 48, 128), vm(30, 48, 128),
        dma((2,)), dma((8,)), dma((8,)), dma((8,)), dma((8,)), dma((31,)), dma((31,)), dma((2, 4)), dma((2, 4)),
        dma((8,)), dma((8,)), dma((31,)), dma((31,)),
    ]
    for X, Y in ((30, 48), (12, 48), (22, 32), (18, 24), (10, 32), (6, 16)):
        scratch += level_scratch(X, Y)
    return pl.pallas_call(
        kernel,
        out_shape=(out, out),
        in_specs=[pl.BlockSpec(memory_space=pltpu.VMEM)] * 2,
        out_specs=(pl.BlockSpec(memory_space=pltpu.VMEM),) * 2,
        scratch_shapes=scratch,
        compiler_params=pltpu.CompilerParams(
            collective_id=0, has_side_effects=True, vmem_limit_bytes=48 * 1024 * 1024
        ),
        name="multigrid",
    )(source, conductivity)


def solution(mesh):
    spec = P("gx", "gy", "gz")
    return jax.shard_map(shards, mesh=mesh, in_specs=(spec, spec), out_specs=(spec, spec), check_vma=False)
```

```python
import jax
import jax.numpy as jnp
from jax import lax
from jax.experimental import pallas as pl
from jax.experimental.pallas import tpu as pltpu
from jax.sharding import PartitionSpec as P

f32 = jnp.float32
MESH = pl.DeviceIdType.MESH

CENTRE = (2.0 + 0.3) / 2.0
HALF = (2.0 - 0.3) / 2.0
SHARP = CENTRE / HALF
W0 = 1.0 / SHARP
W1 = 1.0 / (2.0 * SHARP - W0)
W2 = 1.0 / (2.0 * SHARP - W1)
W3 = 1.0 / (2.0 * SHARP - W2)
B0 = 1.0 / CENTRE
A1, B1 = W1 * W0, 2.0 * W1 / HALF
A2, B2 = W2 * W1, 2.0 * W2 / HALF
A3, B3 = W3 * W2, 2.0 * W3 / HALF

NEAR = [(dx, dy) for dx in (-1, 0, 1) for dy in (-1, 0, 1) if (dx, dy) != (0, 0)]
DIAGONAL = [(dx, dy) for dx, dy in NEAR if dx * dy != 0]


def lanes(rows):
    return lax.broadcasted_iota(jnp.int32, (rows, 128), 1)


def rowid(rows):
    return lax.broadcasted_iota(jnp.int32, (rows, 128), 0)


def gat(x, idx):
    return jnp.take_along_axis(x, idx, axis=1, mode="promise_in_bounds")


def roll(x, shift):
    return pltpu.roll(x, shift, 1)


def loop(lo, hi, width, body):
    def chunk(first, count):
        stores = [st for u in range(count) for st in body(first + u)]
        for ref, index, value in stores:
            ref[index] = value

    def step(j, c):
        chunk(lo + j * width, width)
        return c

    whole = (hi - lo) // width
    if whole == 1:
        chunk(lo, width)
    elif whole > 1:
        lax.fori_loop(0, whole, step, 0)
    if (hi - lo) % width:
        chunk(lo + whole * width, (hi - lo) % width)


def rem(a, n):
    return lax.rem(a, n)


class Level:
    def __init__(self, refs, planes, rows, factor, mask, width):
        self.K, self.R, self.CX, self.CY, self.CZ, self.CW, self.ID, self.VA, self.VB = refs
        self.width = width
        self.X, self.Y, self.h, self.mask = planes, rows, 0.5 * factor, mask

    def clear(self):
        Y = self.Y
        pad = jnp.zeros((8, 128), f32)

        def body(i):
            out = []
            for ref in (self.K, self.VA, self.VB):
                out += [(ref, (i, slice(0, 8)), pad), (ref, (i, slice(8 + Y, 16 + Y)), pad)]
            return out

        loop(0, self.X, 6, body)
        full = jnp.zeros((Y, 128), f32)
        for i in (0, self.X - 1):
            for ref in (self.VA, self.VB, self.K):
                ref[i, 8 : 8 + Y] = full

    def build(self):
        Y, h, K = self.Y, self.h, self.K

        def body(i):
            k = K[i, 8 : 8 + Y]
            low = h * (k + K[i - 1, 8 : 8 + Y])
            high = h * (k + K[i + 1, 8 : 8 + Y])
            cy = h * (K[i, 8 : 16 + Y] + K[i, 7 : 15 + Y])
            cz = h * (k + roll(k, 1))
            cw = h * (k + roll(k, 127))
            ylow = h * (k + K[i, 7 : 7 + Y])
            yhigh = h * (k + K[i, 9 : 9 + Y])
            d = low + high + ylow + yhigh + cz + cw
            inv = jnp.where(self.mask(i), 1.0 / d, 0.0)
            first = B0 * (self.R[i] * inv)
            return [
                (self.CX, i, low), (self.CX, i + 1, high), (self.CY, i, cy), (self.CZ, i, cz), (self.CW, i, cw),
                (self.ID, i, inv), (self.VA, (i, slice(8, 8 + Y)), first),
            ]

        loop(1, self.X - 1, self.width, body)

    def flux(self, V, i):
        Y = self.Y
        v = V[i, 8 : 8 + Y]
        out = self.CX[i] * (v - V[i - 1, 8 : 8 + Y])
        out = out + self.CX[i + 1] * (v - V[i + 1, 8 : 8 + Y])
        out = out + self.CY[i, 0:Y] * (v - V[i, 7 : 7 + Y])
        out = out + self.CY[i, 1 : 1 + Y] * (v - V[i, 9 : 9 + Y])
        out = out + self.CZ[i] * (v - roll(v, 1))
        return v, out + self.CW[i] * (v - roll(v, 127))

    def step(self, src, dst, a, b, shrink, first=False):
        Y = self.Y

        def body(i):
            v, av = self.flux(src, i)
            new = v + b * (self.ID[i] * (self.R[i] - av))
            if first:
                new = new + a * v
            elif a != 0.0:
                new = new + a * (v - dst[i, 8 : 8 + Y])
            return [(dst, (i, slice(8, 8 + Y)), new)]

        loop(1 + shrink, self.X - 1 - shrink, self.width, body)

    def smooth6(self, after=None, trim=True):
        plan = [
            (self.VA, self.VB, A1, B1, True),
            (self.VB, self.VA, A2, B2, False),
            (self.VA, self.VB, 0.0, B0, False),
            (self.VB, self.VA, A1, B1, False),
            (self.VA, self.VB, A2, B2, False),
        ]
        for n, (src, dst, a, b, first) in enumerate(plan):
            self.step(src, dst, a, b, n + 1 if trim else 0, first)
            if after is not None and n < 4:
                after(dst)


def kernel(r_in, k_in, corr_out, res_out, *s):
    (E0, E1, E23, XB, PB, RK2, CB, T, TH, RES, HV, KH, sem_loc, e0s, e0r, e1s, e1r, gs, gr, bs, br, xs, xr, cs, cr, *lv) = s
    gx, gy, gz = lax.axis_index("gx"), lax.axis_index("gy"), lax.axis_index("gz")

    loc = [
        pltpu.make_async_copy(ref, E0.at[n, 7:23, 8:40], sem_loc.at[n]) for n, ref in enumerate((r_in, k_in))
    ]
    for c in loc:
        c.start()

    bar = pltpu.get_barrier_semaphore()

    def inside(dx, dy):
        return (gx + dx >= 0) & (gx + dx < 4) & (gy + dy >= 0) & (gy + dy < 8)

    def greet(dev):
        pl.semaphore_signal(bar, inc=1, device_id=dev, device_id_type=MESH)

    for a in range(1, 4):
        greet({"gx": rem(gx + a, 4)})
    for b in range(1, 8):
        greet({"gy": rem(gy + b, 8)})
    for dx, dy in DIAGONAL:
        pl.when(inside(dx, dy))(lambda dx=dx, dy=dy: greet({"gx": gx + dx, "gy": gy + dy}))

    @pl.when(gz > 0)
    def _():
        greet({"gz": gz - 1})

    @pl.when(gz < 7)
    def _():
        greet({"gz": gz + 1})

    def yz(rows, ylo, ny, zlo, zown, zhi):
        y = rowid(rows) + ylo
        l = lanes(rows)
        low = jnp.where(gz > 0, 128 - zlo, 128)
        high = jnp.where(gz < 7, zown + zhi, zown)
        return (y >= 0) & (y < ny) & ((l < high) | (l >= low))

    def with_x(base, rows, x, nx):
        xv = jnp.zeros((rows, 128), jnp.int32) + x
        return base & (xv >= 0) & (xv < nx)

    def mask0(i):
        return with_x(yz(48, 32 * gy - 8, 256, 0, 128, 0), 48, 16 * gx + i - 7, 64)

    def group(rows):
        l = lanes(rows)
        g = jnp.where(l >= 84, 2, jnp.where(l >= 42, 1, 0))
        return l, g, l - 42 * g

    def masks(i):
        l, g, zz = group(48)
        y = rowid(48) + (32 * gy - 8)
        x = 10 * g + (16 * gx + i - 8)
        low = jnp.where(gz > 0, 0, 8)
        high = jnp.where(gz < 7, 42, 34)
        return (y >= 0) & (y < 256) & (x >= 0) & (x < 64) & (zz >= low) & (zz < high) & (l < 126)

    def mask1(i):
        return with_x(yz(32, 16 * gy - 8, 128, 8, 64, 8), 32, 8 * gx + i - 7, 32)

    def mask2(i):
        return with_x(yz(24, 8 * gy - 8, 64, 8, 32, 8), 24, 4 * gx + i - 7, 16)

    def mask3(i):
        return yz(32, 0, 32, 16, 16, 16)

    def mask4(i):
        return yz(16, 0, 16, 8, 8, 8)

    L0 = Level(lv[0:9], 30, 48, 1.0, mask0, 8)
    LS = Level(lv[9:18], 12, 48, 1.0, masks, 10)
    L1 = Level(lv[18:27], 22, 32, 2.0, mask1, 10)
    L2 = Level(lv[27:36], 18, 24, 4.0, mask2, 8)
    L3 = Level(lv[36:45], 10, 32, 8.0, mask3, 8)
    L4 = Level(lv[45:54], 6, 16, 16.0, mask4, 4)

    for c in loc:
        c.wait()

    l32 = lanes(32)
    zero32 = jnp.zeros((32, 128), f32)

    def pack0(x, c):
        r8, k8 = (roll(E0[n, 7 + x, 8:40], 8 * x) for n in range(2))
        here, before = (l32 >> 3) == x, (l32 >> 3) == ((x + 15) & 15)
        return (
            jnp.where(here, r8, c[0]),
            jnp.where(here, k8, c[1]),
            jnp.where(before, r8, c[2]),
            jnp.where(before, k8, c[3]),
        )

    packed = (zero32,) * 4
    for x in range(16):
        packed = pack0(x, packed)
    PB[0, 0], PB[0, 1] = packed[0], packed[1]
    PB[1, 0], PB[1, 1] = roll(packed[2], 8), roll(packed[3], 8)

    def pair(x, rows):
        l = lanes(rows)
        return gat(x, (2 * l) & 127) + gat(x, (2 * l + 1) & 127)

    l16 = lanes(16)

    def down1(x, c):
        out = []
        for n in range(2):
            a, b = (E0[n, 7 + 2 * x + p, pl.ds(8, 16, stride=2)] + E0[n, 7 + 2 * x + p, pl.ds(9, 16, stride=2)] for p in range(2))
            t = a + b
            out.append(pair(t, 16))
        rk = jnp.where(l16 < 64, out[0], 0.125 * out[1])
        E1[7 + x, 8:24] = rk
        here = ((l16 & 63) >> 3) == x
        return (
            jnp.where(here, roll(rk, 8 * x), c[0]),
            jnp.where(here, roll(rk, (8 * x + 72) & 127), c[1]),
        )

    zero16 = jnp.zeros((16, 128), f32)
    low1 = high1 = zero16
    for x in range(8):
        low1, high1 = down1(x, (low1, high1))
    for side, val in enumerate((low1, high1)):
        PB[side, 2, 0:8] = val[0:8]
        PB[side, 2, 24:32] = val[8:16]

    l8 = lanes(8)
    zero8 = jnp.zeros((8, 128), f32)

    def down2(x, c):
        def part(p, n):
            return E1[7 + 2 * x + p, pl.ds(8 + n, 8, stride=2)]

        t = (part(0, 0) + part(0, 1)) + (part(1, 0) + part(1, 1))
        rk = pair(t, 8)
        rk = jnp.where(((l8 >> 5) & 1) == 1, 0.125 * rk, rk)
        RK2[x] = rk
        here, edge = (l8 >> 5) == x, (l8 < 64) & (((l8 & 31) >> 3) == x)
        return (
            jnp.where(here, roll(rk, 32 * x), c[0]),
            jnp.where(here, roll(rk, (32 * x + 96) & 127), c[1]),
            jnp.where(edge, roll(rk, 8 * x), c[2]),
            jnp.where(edge, roll(rk, (8 * x + 104) & 127), c[3]),
        )

    r2 = k2 = low2 = high2 = zero8
    for x in range(4):
        r2, k2, low2, high2 = down2(x, (r2, k2, low2, high2))
    l4 = lanes(4)
    rk3 = []
    for x in range(2):
        t = (RK2[2 * x, pl.ds(0, 4, stride=2)] + RK2[2 * x, pl.ds(1, 4, stride=2)]) + (
            RK2[2 * x + 1, pl.ds(0, 4, stride=2)] + RK2[2 * x + 1, pl.ds(1, 4, stride=2)]
        )
        T[x, 0:4], T[x, 4:8] = t, t
        t = pair(T[x, 0:8], 8)
        rk3.append(jnp.where(((l8 >> 4) & 1) == 1, 0.125 * t, t))
    m3 = jnp.where(((l8 >> 5) & 1) == 0, rk3[0], rk3[1])
    E23[gy, gx, 0], E23[gy, gx, 1] = r2, k2
    RK2[0] = jnp.where(l8 < 64, low2, m3)
    RK2[1] = jnp.where(l8 < 64, high2, m3)

    for L in (L0, LS, L1, L2, L3, L4):
        L.clear()

    def sides(at, n):
        return jnp.where(at > 0, 1, 0) + jnp.where(at < n - 1, 1, 0)

    pl.semaphore_wait(bar, 10 + sides(gx, 4) * sides(gy, 8) + sides(gz, 8))

    def zcopies(side):
        dev = {"gz": gz - 1 if side == 0 else gz + 1}
        land = 1 - side
        pieces = [
            (RK2.at[side], CB.at[land]),
            (PB.at[side, 2, 0:8], XB.at[1, land, 2, 8:16]),
            (PB.at[side, 2, 24:32], XB.at[1, land, 2, 32:40]),
            (PB.at[side, 0:2], XB.at[1, land, 0:2, 8:40]),
        ]
        return [
            pltpu.make_async_remote_copy(
                src_ref=src, dst_ref=dst, send_sem=bs.at[side, n], recv_sem=br.at[side, n],
                device_id=dev, device_id_type=MESH,
            )
            for n, (src, dst) in enumerate(pieces)
        ]

    def each(cond, copies, what):
        @pl.when(cond)
        def _():
            for c in copies:
                getattr(c, what)()

    zdown, zup = zcopies(0), zcopies(1)
    each(gz > 0, zdown, "start")
    each(gz < 7, zup, "start")

    SRC0X, DST0X = {-1: (7, 14), 0: (7, 23), 1: (16, 23)}, {-1: (23, 30), 0: (7, 23), 1: (0, 7)}
    SRC0Y, DST0Y = {-1: (8, 16), 0: (8, 40), 1: (32, 40)}, {-1: (40, 48), 0: (8, 40), 1: (0, 8)}
    SRC1X, DST1X = {-1: (7, 14), 0: (7, 15), 1: (8, 15)}, {-1: (15, 22), 0: (7, 15), 1: (0, 7)}
    SRC1Y, DST1Y = {-1: (8, 16), 0: (8, 24), 1: (16, 24)}, {-1: (24, 32), 0: (8, 24), 1: (0, 8)}

    def sl(pairs):
        return pl.ds(pairs[0], pairs[1] - pairs[0])

    def near_copies(make):
        return [(inside(dx, dy), inside(-dx, -dy), make(n, dx, dy)) for n, (dx, dy) in enumerate(NEAR)]

    def rc(src, dst, ss, rs, dev):
        return pltpu.make_async_remote_copy(
            src_ref=src, dst_ref=dst, send_sem=ss, recv_sem=rs, device_id=dev, device_id_type=MESH
        )

    def dev_near(dx, dy):
        return {"gx": gx + dx, "gy": gy + dy}

    c0 = near_copies(lambda n, dx, dy: rc(
        E0.at[:, sl(SRC0X[dx]), sl(SRC0Y[dy])], E0.at[:, sl(DST0X[dx]), sl(DST0Y[dy])], e0s.at[n], e0r.at[n], dev_near(dx, dy)))
    c1 = near_copies(lambda n, dx, dy: rc(
        E1.at[sl(SRC1X[dx]), sl(SRC1Y[dy])], E1.at[sl(DST1X[dx]), sl(DST1Y[dy])], e1s.at[n], e1r.at[n], dev_near(dx, dy)))
    def slab_copies(first, last, base):
        return near_copies(lambda n, dx, dy: rc(
            XB.at[1, :, first:last, sl(SRC0Y[dy])], XB.at[1 - dx, :, first:last, sl(DST0Y[dy])],
            xs.at[base + n], xr.at[base + n], dev_near(dx, dy)))

    cx1, cx0 = slab_copies(2, 3, 0), slab_copies(0, 2, 8)

    gather_x = [
        rc(E23.at[gy, gx], E23.at[gy, gx], gs.at[a - 1], gr.at[a - 1], {"gx": rem(gx + a, 4)}) for a in range(1, 4)
    ]
    gather_y = []
    for b in range(1, 8):
        dev = {"gy": rem(gy + b, 8)}
        wide = rc(E23.at[gy], E23.at[gy], cs.at[b - 1], cr.at[b - 1], dev)
        thin = rc(E23.at[gy, :, 3:4], E23.at[gy, :, 3:4], cs.at[b - 1], cr.at[b - 1], dev)
        to = gy < 7 if b == 1 else gy > 0 if b == 7 else None
        of = gy > 0 if b == 1 else gy < 7 if b == 7 else None
        gather_y.append((wide, thin, to, of))

    def each_y(what, end):
        for wide, thin, to, of in gather_y:
            cond = of if end else to
            if cond is None:
                getattr(thin, what)()
            else:
                each(cond, [wide], what)
                each(jnp.logical_not(cond), [thin], what)

    for ok, _, c in c0 + c1:
        each(ok, [c], "start")

    @pl.when(gz == 0)
    def _():
        for n in range(3):
            XB[1, 0, n, 8:40] = zero32
        CB[0] = zero8

    @pl.when(gz == 7)
    def _():
        for n in range(3):
            XB[1, 1, n, 8:40] = zero32
        CB[1] = zero8

    each(gz < 7, zdown[0:1], "wait_recv")
    each(gz > 0, zup[0:1], "wait_recv")
    top = rowid(8) < 4
    E23[gy, gx, 2] = jnp.where(l8 < 64, CB[0], roll(CB[1], 64))
    E23[gy, gx, 3] = jnp.where(l8 < 64, m3, jnp.where(top, CB[0], CB[1]))
    for c in gather_x:
        c.start()
    each(gz < 7, zdown[1:3], "wait_recv")
    each(gz > 0, zup[1:3], "wait_recv")
    for ok, _, c in cx1:
        each(ok, [c], "start")

    for _, okr, c in c0:
        each(okr, [c], "wait_recv")

    def load0(i):
        m = mask0(i)
        return [
            (L0.K, (i, slice(8, 56)), jnp.where(m, E0[1, i], 0.0)), (L0.R, i, jnp.where(m, E0[0, i], 0.0)),
        ]

    loop(0, 30, 6, load0)
    L0.build()
    for c in gather_x:
        c.wait_recv()
    each_y("start", False)
    each(gz < 7, zdown[3:4], "wait_recv")
    each(gz > 0, zup[3:4], "wait_recv")
    for ok, _, c in cx0:
        each(ok, [c], "start")
    L0.smooth6()

    each_y("wait_recv", True)
    in3 = yz(8, 0, 8, 16, 16, 16)
    for sx in range(4):
        def load3(q, sx=sx):
            a, b = E23[2 * q, sx, 3], E23[2 * q + 1, sx, 3]
            m = jnp.where(top, a, b)
            lo = jnp.where(top, a, pltpu.roll(b, 4, 0))
            hi = jnp.where(top, pltpu.roll(a, 4, 0), b)
            out3 = []
            for xl in range(2):
                for isk in range(2):
                    at = 32 * xl + 16 * isk
                    out = jnp.where(
                        l8 < 16, roll(m, (128 - at) % 128),
                        jnp.where(l8 < 32, roll(hi, (16 - 64 - at) % 128), roll(lo, (112 - 64 - at) % 128)),
                    )
                    out = jnp.where(in3, out, 0.0)
                    plane = 1 + 2 * sx + xl
                    if isk:
                        out3.append((L3.K, (plane, slice(8 + 8 * q, 16 + 8 * q)), out))
                    else:
                        out3.append((L3.R, (plane, slice(8 * q, 8 * q + 8)), out))
            return out3

        loop(0, 4, 4, load3)
    L3.build()
    L3.step(L3.VA, L3.VB, A1, B1, 0, True)

    def residue(i):
        _, av = L3.flux(L3.VB, i)
        return [(RES, i - 1, L3.R[i] - av)]

    loop(1, 9, 4, residue)
    in4 = mask4(0)

    def down4(x):
        t = (RES[2 * x, pl.ds(0, 16, stride=2)] + RES[2 * x, pl.ds(1, 16, stride=2)]) + (
            RES[2 * x + 1, pl.ds(0, 16, stride=2)] + RES[2 * x + 1, pl.ds(1, 16, stride=2)]
        )
        r4 = jnp.where(in4, pair(t, 16), 0.0)
        t = (L3.K[1 + 2 * x, pl.ds(8, 16, stride=2)] + L3.K[1 + 2 * x, pl.ds(9, 16, stride=2)]) + (
            L3.K[2 + 2 * x, pl.ds(8, 16, stride=2)] + L3.K[2 + 2 * x, pl.ds(9, 16, stride=2)]
        )
        k4 = jnp.where(in4, 0.125 * pair(t, 16), 0.0)
        return [(L4.R, 1 + x, r4), (L4.K, (1 + x, slice(8, 24)), k4)]

    loop(0, 4, 4, down4)
    L4.build()
    L4.step(L4.VA, L4.VB, A1, B1, 0, True)
    L4.step(L4.VB, L4.VA, A2, B2, 0)
    L4.step(L4.VA, L4.VB, A3, B3, 0)

    def repeat_lanes(x, rows):
        l = lanes(rows)
        return gat(x, jnp.where(l < 96, l >> 1, (l >> 1) + 64))

    def repeat_rows(ref, slot, x, rows):
        ref[slot, pl.ds(0, rows, stride=2)] = x
        ref[slot, pl.ds(1, rows, stride=2)] = x
        return ref[slot, 0 : 2 * rows]

    def up4(x):
        t = repeat_rows(T, x, repeat_lanes(L4.VB[1 + x, 8:24], 16), 16)
        rows = slice(8, 40)
        return [(L3.VB, (1 + 2 * x + p, rows), L3.VB[1 + 2 * x + p, rows] + t) for p in range(2)]

    loop(0, 4, 4, up4)
    L3.step(L3.VB, L3.VA, 0.0, B0, 0)
    L3.step(L3.VA, L3.VB, A1, B1, 0)

    def load2(i):
        xg = 4 * gx + i - 7 + 8
        sx = (xg >> 2) - 2
        xl = xg & 3
        scx = jnp.clip(sx, 0, 3)
        m = mask2(i)
        out2 = []
        for n in range(3):
            sy = jnp.clip(gy + n - 1, 0, 7)
            r, k, edge = E23[sy, scx, 0], E23[sy, scx, 1], E23[sy, scx, 2]
            mn = m[8 * n : 8 * n + 8]
            for isk, mid in ((0, r), (1, k)):
                at = 8 * xl + 32 * isk
                out = jnp.where(
                    l8 < 32, roll(mid, (128 - 32 * xl) & 127),
                    jnp.where(l8 < 64, roll(edge, (224 - at) & 127), roll(edge, (248 - at) & 127)),
                )
                out = jnp.where(mn, out, 0.0)
                if isk:
                    out2.append((L2.K, (i, slice(8 + 8 * n, 16 + 8 * n)), out))
                else:
                    out2.append((L2.R, (i, slice(8 * n, 8 * n + 8)), out))
        return out2

    loop(0, 18, 6, load2)
    L2.build()
    L2.smooth6()

    def up3(q):
        w = L3.VB[2 * gx + q, pl.ds(4 * gy + 4, 16)]
        t = repeat_rows(T, 4 + q, repeat_lanes(w, 16), 16)[0:24]
        rows = slice(8, 32)
        return [(L2.VB, (2 * q + 5 + p, rows), L2.VB[2 * q + 5 + p, rows] + t) for p in range(2)]

    loop(0, 4, 4, up3)

    for _, okr, c in c1 + cx1:
        each(okr, [c], "wait_recv")

    l32b = lanes(32)

    def load1(i):
        x = i - 7
        dx = jnp.where(x >= 0, 1, 0) + jnp.where(x >= 8, 1, 0)
        xl = x & 7
        m = mask1(i)
        main = E1[i]
        out1 = []
        lo = jnp.concatenate([XB[dx, 0, 2, 0:16], XB[dx, 0, 2, 32:48]], axis=0)
        hi = jnp.concatenate([XB[dx, 1, 2, 0:16], XB[dx, 1, 2, 32:48]], axis=0)
        for isk in range(2):
            at = 8 * xl + 64 * isk
            mid = roll(main, 64) if isk else main
            out = jnp.where(
                l32b < 64, mid,
                jnp.where(l32b < 96, roll(hi, (192 - at) & 127), roll(lo, (248 - at) & 127)),
            )
            out = jnp.where(m, out, 0.0)
            if isk:
                out1.append((L1.K, (i, slice(8, 40)), out))
            else:
                out1.append((L1.R, i, out))
        return out1

    loop(0, 22, 4, load1)
    L1.build()
    L1.smooth6()

    def up2(q):
        t = repeat_rows(T, 8 + q, repeat_lanes(L2.VB[q + 6, 12:28], 16), 16)
        rows = slice(8, 40)
        return [(L1.VB, (2 * q + 5 + p, rows), L1.VB[2 * q + 5 + p, rows] + t) for p in range(2)]

    loop(0, 6, 6, up2)

    for _, okr, c in cx0:
        each(okr, [c], "wait_recv")
    ls, gsl, zz = group(48)

    def load_slab(xi):
        m = masks(xi + 1)
        x = 10 * gsl + (xi - 7)
        which = jnp.where(x >= 0, 1, 0) + jnp.where(x >= 16, 1, 0)
        xl = x & 15
        ilo = (8 * xl + zz) & 127
        ihi = (8 * xl + zz - 34) & 127
        imain = jnp.where(zz < 21, zz - 8, zz + 94) & 127
        outs = []
        for arr in range(2):
            src = L0.K if arr else L0.R
            parts = []
            for g in range(3):
                plane = src[10 * g + xi, 8:56] if arr else src[10 * g + xi]
                parts.append(gat(plane, imain))
            mid = jnp.where(gsl == 0, parts[0], jnp.where(gsl == 1, parts[1], parts[2]))
            lo = [gat(XB[d, 0, arr], ilo) for d in range(3)]
            hi = [gat(XB[d, 1, arr], ihi) for d in range(3)]
            pick = [jnp.where(which == 0, t[0], jnp.where(which == 1, t[1], t[2])) for t in (lo, hi)]
            out = jnp.where(zz < 8, pick[0], jnp.where(zz >= 34, pick[1], mid))
            out = jnp.where(m, out, 0.0)
            if arr:
                outs.append((LS.K, (1 + xi, slice(8, 56)), out))
            else:
                outs.append((LS.R, 1 + xi, out))
        return outs

    loop(0, 10, 2, load_slab)

    def ghosts(ref):
        ref[0, 8:56] = roll(ref[10, 8:56], 42)
        ref[11, 8:56] = roll(ref[1, 8:56], 86)

    ghosts(LS.K)
    LS.build()
    ghosts(LS.VA)
    LS.smooth6(after=ghosts, trim=False)

    l48, l24 = lanes(48), lanes(24)

    def merge(q):
        w = L1.VB[q + 6, 12:36]
        t = repeat_rows(T, 14 + q, gat(w, l24 >> 1), 24)
        th = repeat_rows(TH, q, gat(w, jnp.where(l24 == 0, 127, 64)), 24)
        out = []
        for p in range(2):
            i = 2 * q + 5 + p
            g = jnp.where(i >= 10, 1, 0) + jnp.where(i >= 20, 1, 0)
            xi = i - 10 * g
            sv = LS.VB[1 + xi, 8:56]
            sk = LS.K[1 + xi, 8:56]
            off = 42 * g
            v = jnp.where(
                l48 < 6, roll(sv, (248 - off) & 127),
                jnp.where(l48 >= 122, roll(sv, (222 - off) & 127), L0.VB[i, 8:56]),
            )
            hv = jnp.where(l48 < 64, roll(sv, (249 - off) & 127), roll(sv, (221 - off) & 127)) + th
            kh = jnp.where(l48 < 64, roll(sk, (249 - off) & 127), roll(sk, (221 - off) & 127))
            out += [(L0.VB, (i, slice(8, 56)), v + t), (HV, i, hv), (KH, i, kh)]
        return out

    loop(0, 10, 2, merge)

    def final(x):
        i = x + 7
        c = slice(16, 48)
        v = L0.VB[i, c]
        k = L0.K[i, c]
        hv, kh = HV[i, 8:40], KH[i, 8:40]
        out = L0.CX[i, 8:40] * (v - L0.VB[i - 1, c])
        out = out + L0.CX[i + 1, 8:40] * (v - L0.VB[i + 1, c])
        out = out + L0.CY[i, 8:40] * (v - L0.VB[i, 15:47])
        out = out + L0.CY[i, 9:41] * (v - L0.VB[i, 17:49])
        cl = 0.5 * (k + jnp.where(l32 == 0, kh, roll(k, 1)))
        cr = 0.5 * (k + jnp.where(l32 == 127, kh, roll(k, 127)))
        out = out + cl * (v - jnp.where(l32 == 0, hv, roll(v, 1)))
        out = out + cr * (v - jnp.where(l32 == 127, hv, roll(v, 127)))
        return [(corr_out, x, v), (res_out, x, E0[0, i, 8:40] - out)]

    loop(0, 16, 4, final)

    each(gz > 0, zdown, "wait_send")
    each(gz < 7, zup, "wait_send")
    for ok, _, c in c0 + c1 + cx0 + cx1:
        each(ok, [c], "wait_send")
    for c in gather_x:
        c.wait_send()
    each_y("wait_send", False)


def level_scratch(X, Y):
    big, mid = pltpu.VMEM((X, Y + 16, 128), f32), pltpu.VMEM((X, Y, 128), f32)
    return [big, mid, mid, pltpu.VMEM((X, Y + 8, 128), f32), mid, mid, mid, big, big]


def shards(source, conductivity):
    dma = pltpu.SemaphoreType.DMA
    vm = lambda *shape: pltpu.VMEM(shape, f32)
    out = jax.ShapeDtypeStruct((16, 32, 128), f32)
    scratch = [
        vm(2, 30, 48, 128), vm(22, 32, 128), vm(8, 4, 4, 8, 128), vm(3, 2, 3, 48, 128), vm(2, 3, 32, 128),
        vm(4, 8, 128), vm(2, 8, 128), vm(24, 48, 128), vm(10, 48, 128), vm(8, 32, 128), vm(30, 48, 128), vm(30, 48, 128),
        dma((2,)), dma((8,)), dma((8,)), dma((8,)), dma((8,)), dma((3,)), dma((3,)), dma((2, 4)), dma((2, 4)),
        dma((16,)), dma((16,)), dma((7,)), dma((7,)),
    ]
    for X, Y in ((30, 48), (12, 48), (22, 32), (18, 24), (10, 32), (6, 16)):
        scratch += level_scratch(X, Y)
    return pl.pallas_call(
        kernel,
        out_shape=(out, out),
        in_specs=[pl.BlockSpec(memory_space=pltpu.HBM)] * 2,
        out_specs=(pl.BlockSpec(memory_space=pltpu.VMEM),) * 2,
        scratch_shapes=scratch,
        compiler_params=pltpu.CompilerParams(
            collective_id=0, has_side_effects=True, vmem_limit_bytes=48 * 1024 * 1024
        ),
        name="multigrid",
    )(source, conductivity)


def solution(mesh):
    spec = P("gx", "gy", "gz")
    return jax.shard_map(shards, mesh=mesh, in_specs=(spec, spec), out_specs=(spec, spec), check_vma=False)
```

```python
import jax
import jax.numpy as jnp
from jax import lax
from jax.experimental import pallas as pl
from jax.experimental.pallas import tpu as pltpu
from jax.sharding import PartitionSpec as P

f32 = jnp.float32
MESH = pl.DeviceIdType.MESH

CENTRE = (2.0 + 0.3) / 2.0
HALF = (2.0 - 0.3) / 2.0
SHARP = CENTRE / HALF
W0 = 1.0 / SHARP
W1 = 1.0 / (2.0 * SHARP - W0)
W2 = 1.0 / (2.0 * SHARP - W1)
W3 = 1.0 / (2.0 * SHARP - W2)
B0 = 1.0 / CENTRE
A1, B1 = W1 * W0, 2.0 * W1 / HALF
A2, B2 = W2 * W1, 2.0 * W2 / HALF
A3, B3 = W3 * W2, 2.0 * W3 / HALF

NEAR = [(dx, dy) for dx in (-1, 0, 1) for dy in (-1, 0, 1) if (dx, dy) != (0, 0)]
DIAGONAL = [(dx, dy) for dx, dy in NEAR if dx * dy != 0]


def lanes(rows):
    return lax.broadcasted_iota(jnp.int32, (rows, 128), 1)


def rowid(rows):
    return lax.broadcasted_iota(jnp.int32, (rows, 128), 0)


def gat(x, idx):
    return jnp.take_along_axis(x, idx, axis=1, mode="promise_in_bounds")


def roll(x, shift):
    return pltpu.roll(x, shift, 1)


def loop(lo, hi, width, body):
    def chunk(first, count):
        stores = [st for u in range(count) for st in body(first + u)]
        for ref, index, value in stores:
            ref[index] = value

    def step(j, c):
        chunk(lo + j * width, width)
        return c

    whole = (hi - lo) // width
    if whole == 1:
        chunk(lo, width)
    elif whole > 1:
        lax.fori_loop(0, whole, step, 0)
    if (hi - lo) % width:
        chunk(lo + whole * width, (hi - lo) % width)


def rem(a, n):
    return lax.rem(a, n)


class Level:
    def __init__(self, refs, planes, rows, factor, mask, width):
        self.K, self.R, self.CX, self.CY, self.CZ, self.CW, self.ID, self.VA, self.VB = refs
        self.width = width
        self.X, self.Y, self.h, self.mask = planes, rows, 0.5 * factor, mask

    def clear(self):
        Y = self.Y
        pad = jnp.zeros((8, 128), f32)

        def body(i):
            out = []
            for ref in (self.K, self.VA, self.VB):
                out += [(ref, (i, slice(0, 8)), pad), (ref, (i, slice(8 + Y, 16 + Y)), pad)]
            return out

        loop(0, self.X, 6, body)
        full = jnp.zeros((Y, 128), f32)
        for i in (0, self.X - 1):
            for ref in (self.VA, self.VB, self.K):
                ref[i, 8 : 8 + Y] = full

    def build(self):
        Y, h, K = self.Y, self.h, self.K

        def body(i):
            k = K[i, 8 : 8 + Y]
            low = h * (k + K[i - 1, 8 : 8 + Y])
            high = h * (k + K[i + 1, 8 : 8 + Y])
            cy = h * (K[i, 8 : 16 + Y] + K[i, 7 : 15 + Y])
            cz = h * (k + roll(k, 1))
            cw = h * (k + roll(k, 127))
            ylow = h * (k + K[i, 7 : 7 + Y])
            yhigh = h * (k + K[i, 9 : 9 + Y])
            d = low + high + ylow + yhigh + cz + cw
            inv = jnp.where(self.mask(i), 1.0 / d, 0.0)
            first = B0 * (self.R[i] * inv)
            return [
                (self.CX, i, low), (self.CX, i + 1, high), (self.CY, i, cy), (self.CZ, i, cz), (self.CW, i, cw),
                (self.ID, i, inv), (self.VA, (i, slice(8, 8 + Y)), first),
            ]

        loop(1, self.X - 1, self.width, body)

    def flux(self, V, i):
        Y = self.Y
        v = V[i, 8 : 8 + Y]
        out = self.CX[i] * (v - V[i - 1, 8 : 8 + Y])
        out = out + self.CX[i + 1] * (v - V[i + 1, 8 : 8 + Y])
        out = out + self.CY[i, 0:Y] * (v - V[i, 7 : 7 + Y])
        out = out + self.CY[i, 1 : 1 + Y] * (v - V[i, 9 : 9 + Y])
        out = out + self.CZ[i] * (v - roll(v, 1))
        return v, out + self.CW[i] * (v - roll(v, 127))

    def step(self, src, dst, a, b, shrink, first=False):
        Y = self.Y

        def body(i):
            v, av = self.flux(src, i)
            new = v + b * (self.ID[i] * (self.R[i] - av))
            if first:
                new = new + a * v
            elif a != 0.0:
                new = new + a * (v - dst[i, 8 : 8 + Y])
            return [(dst, (i, slice(8, 8 + Y)), new)]

        loop(1 + shrink, self.X - 1 - shrink, self.width, body)

    def smooth6(self, after=None, trim=True):
        plan = [
            (self.VA, self.VB, A1, B1, True),
            (self.VB, self.VA, A2, B2, False),
            (self.VA, self.VB, 0.0, B0, False),
            (self.VB, self.VA, A1, B1, False),
            (self.VA, self.VB, A2, B2, False),
        ]
        for n, (src, dst, a, b, first) in enumerate(plan):
            self.step(src, dst, a, b, n + 1 if trim else 0, first)
            if after is not None and n < 4:
                after(dst)


def kernel(r_in, k_in, corr_out, res_out, *s):
    (E0, E1, E23, XB, PB, RK2, CB, T, TH, RES, HV, KH, sem_loc, e0s, e0r, e1s, e1r, gs, gr, bs, br, xs, xr, cs, cr, *lv) = s
    gx, gy, gz = lax.axis_index("gx"), lax.axis_index("gy"), lax.axis_index("gz")

    loc = [
        pltpu.make_async_copy(ref, E0.at[n, 7:23, 8:40], sem_loc.at[n]) for n, ref in enumerate((r_in, k_in))
    ]
    for c in loc:
        c.start()

    bar = pltpu.get_barrier_semaphore()

    def inside(dx, dy):
        return (gx + dx >= 0) & (gx + dx < 4) & (gy + dy >= 0) & (gy + dy < 8)

    def greet(dev):
        pl.semaphore_signal(bar, inc=1, device_id=dev, device_id_type=MESH)

    @pl.when(gz > 0)
    def _():
        greet({"gz": gz - 1})

    @pl.when(gz < 7)
    def _():
        greet({"gz": gz + 1})

    for a in range(1, 4):
        greet({"gx": rem(gx + a, 4)})
    for b in range(1, 8):
        greet({"gy": rem(gy + b, 8)})
    for dx, dy in DIAGONAL:
        pl.when(inside(dx, dy))(lambda dx=dx, dy=dy: greet({"gx": gx + dx, "gy": gy + dy}))

    def yz(rows, ylo, ny, zlo, zown, zhi):
        y = rowid(rows) + ylo
        l = lanes(rows)
        low = jnp.where(gz > 0, 128 - zlo, 128)
        high = jnp.where(gz < 7, zown + zhi, zown)
        return (y >= 0) & (y < ny) & ((l < high) | (l >= low))

    def with_x(base, rows, x, nx):
        xv = jnp.zeros((rows, 128), jnp.int32) + x
        return base & (xv >= 0) & (xv < nx)

    def mask0(i):
        return with_x(yz(48, 32 * gy - 8, 256, 0, 128, 0), 48, 16 * gx + i - 7, 64)

    def group(rows):
        l = lanes(rows)
        g = jnp.where(l >= 84, 2, jnp.where(l >= 42, 1, 0))
        return l, g, l - 42 * g

    def masks(i):
        l, g, zz = group(48)
        y = rowid(48) + (32 * gy - 8)
        x = 10 * g + (16 * gx + i - 8)
        low = jnp.where(gz > 0, 0, 8)
        high = jnp.where(gz < 7, 42, 34)
        return (y >= 0) & (y < 256) & (x >= 0) & (x < 64) & (zz >= low) & (zz < high) & (l < 126)

    def mask1(i):
        return with_x(yz(32, 16 * gy - 8, 128, 8, 64, 8), 32, 8 * gx + i - 7, 32)

    def mask2(i):
        return with_x(yz(24, 8 * gy - 8, 64, 8, 32, 8), 24, 4 * gx + i - 7, 16)

    def mask3(i):
        return yz(32, 0, 32, 16, 16, 16)

    def mask4(i):
        return yz(16, 0, 16, 8, 8, 8)

    L0 = Level(lv[0:9], 30, 48, 1.0, mask0, 8)
    LS = Level(lv[9:18], 12, 48, 1.0, masks, 10)
    L1 = Level(lv[18:27], 22, 32, 2.0, mask1, 10)
    L2 = Level(lv[27:36], 18, 24, 4.0, mask2, 8)
    L3 = Level(lv[36:45], 10, 32, 8.0, mask3, 8)
    L4 = Level(lv[45:54], 6, 16, 16.0, mask4, 4)

    for c in loc:
        c.wait()

    l32 = lanes(32)
    zero32 = jnp.zeros((32, 128), f32)

    def pack0(x, c):
        r8, k8 = (roll(E0[n, 7 + x, 8:40], 8 * x) for n in range(2))
        here, before = (l32 >> 3) == x, (l32 >> 3) == ((x + 15) & 15)
        return (
            jnp.where(here, r8, c[0]),
            jnp.where(here, k8, c[1]),
            jnp.where(before, r8, c[2]),
            jnp.where(before, k8, c[3]),
        )

    packed = (zero32,) * 4
    for x in range(16):
        packed = pack0(x, packed)
    PB[0, 0], PB[0, 1] = packed[0], packed[1]
    PB[1, 0], PB[1, 1] = roll(packed[2], 8), roll(packed[3], 8)

    def pair(x, rows):
        l = lanes(rows)
        return gat(x, (2 * l) & 127) + gat(x, (2 * l + 1) & 127)

    l16 = lanes(16)

    def down1(x, c):
        out = []
        for n in range(2):
            a, b = (E0[n, 7 + 2 * x + p, pl.ds(8, 16, stride=2)] + E0[n, 7 + 2 * x + p, pl.ds(9, 16, stride=2)] for p in range(2))
            t = a + b
            out.append(pair(t, 16))
        rk = jnp.where(l16 < 64, out[0], 0.125 * out[1])
        E1[7 + x, 8:24] = rk
        here = ((l16 & 63) >> 3) == x
        return (
            jnp.where(here, roll(rk, 8 * x), c[0]),
            jnp.where(here, roll(rk, (8 * x + 72) & 127), c[1]),
        )

    zero16 = jnp.zeros((16, 128), f32)
    low1 = high1 = zero16
    for x in range(8):
        low1, high1 = down1(x, (low1, high1))
    for side, val in enumerate((low1, high1)):
        PB[side, 2, 0:8] = val[0:8]
        PB[side, 2, 24:32] = val[8:16]

    l8 = lanes(8)
    zero8 = jnp.zeros((8, 128), f32)

    def down2(x, c):
        def part(p, n):
            return E1[7 + 2 * x + p, pl.ds(8 + n, 8, stride=2)]

        t = (part(0, 0) + part(0, 1)) + (part(1, 0) + part(1, 1))
        rk = pair(t, 8)
        rk = jnp.where(((l8 >> 5) & 1) == 1, 0.125 * rk, rk)
        RK2[x] = rk
        here, edge = (l8 >> 5) == x, (l8 < 64) & (((l8 & 31) >> 3) == x)
        return (
            jnp.where(here, roll(rk, 32 * x), c[0]),
            jnp.where(here, roll(rk, (32 * x + 96) & 127), c[1]),
            jnp.where(edge, roll(rk, 8 * x), c[2]),
            jnp.where(edge, roll(rk, (8 * x + 104) & 127), c[3]),
        )

    r2 = k2 = low2 = high2 = zero8
    for x in range(4):
        r2, k2, low2, high2 = down2(x, (r2, k2, low2, high2))
    l4 = lanes(4)
    rk3 = []
    for x in range(2):
        t = (RK2[2 * x, pl.ds(0, 4, stride=2)] + RK2[2 * x, pl.ds(1, 4, stride=2)]) + (
            RK2[2 * x + 1, pl.ds(0, 4, stride=2)] + RK2[2 * x + 1, pl.ds(1, 4, stride=2)]
        )
        T[x, 0:4], T[x, 4:8] = t, t
        t = pair(T[x, 0:8], 8)
        rk3.append(jnp.where(((l8 >> 4) & 1) == 1, 0.125 * t, t))
    m3 = jnp.where(((l8 >> 5) & 1) == 0, rk3[0], rk3[1])
    E23[gy, gx, 0], E23[gy, gx, 1] = r2, k2
    RK2[0] = jnp.where(l8 < 64, low2, m3)
    RK2[1] = jnp.where(l8 < 64, high2, m3)

    for L in (L0, LS, L1, L2, L3, L4):
        L.clear()

    def sides(at, n):
        return jnp.where(at > 0, 1, 0) + jnp.where(at < n - 1, 1, 0)

    pl.semaphore_wait(bar, 10 + sides(gx, 4) * sides(gy, 8) + sides(gz, 8))

    def zcopies(side):
        dev = {"gz": gz - 1 if side == 0 else gz + 1}
        land = 1 - side
        pieces = [
            (RK2.at[side], CB.at[land]),
            (PB.at[side, 2, 0:8], XB.at[1, land, 2, 8:16]),
            (PB.at[side, 2, 24:32], XB.at[1, land, 2, 32:40]),
            (PB.at[side, 0:2], XB.at[1, land, 0:2, 8:40]),
        ]
        return [
            pltpu.make_async_remote_copy(
                src_ref=src, dst_ref=dst, send_sem=bs.at[side, n], recv_sem=br.at[side, n],
                device_id=dev, device_id_type=MESH,
            )
            for n, (src, dst) in enumerate(pieces)
        ]

    def each(cond, copies, what):
        @pl.when(cond)
        def _():
            for c in copies:
                getattr(c, what)()

    zdown, zup = zcopies(0), zcopies(1)
    each(gz > 0, zdown, "start")
    each(gz < 7, zup, "start")

    SRC0X, DST0X = {-1: (7, 14), 0: (7, 23), 1: (16, 23)}, {-1: (23, 30), 0: (7, 23), 1: (0, 7)}
    SRC0Y, DST0Y = {-1: (8, 16), 0: (8, 40), 1: (32, 40)}, {-1: (40, 48), 0: (8, 40), 1: (0, 8)}
    SRC1X, DST1X = {-1: (7, 14), 0: (7, 15), 1: (8, 15)}, {-1: (15, 22), 0: (7, 15), 1: (0, 7)}
    SRC1Y, DST1Y = {-1: (8, 16), 0: (8, 24), 1: (16, 24)}, {-1: (24, 32), 0: (8, 24), 1: (0, 8)}

    def sl(pairs):
        return pl.ds(pairs[0], pairs[1] - pairs[0])

    def near_copies(make):
        return [(inside(dx, dy), inside(-dx, -dy), make(n, dx, dy)) for n, (dx, dy) in enumerate(NEAR)]

    def rc(src, dst, ss, rs, dev):
        return pltpu.make_async_remote_copy(
            src_ref=src, dst_ref=dst, send_sem=ss, recv_sem=rs, device_id=dev, device_id_type=MESH
        )

    def dev_near(dx, dy):
        return {"gx": gx + dx, "gy": gy + dy}

    def thinner(pairs, dx, dy):
        if dx == 0 or dy == 0:
            return sl(pairs)
        return sl((pairs[0] + 1, pairs[1])) if dx == 1 else sl((pairs[0], pairs[1] - 1))

    c0 = near_copies(lambda n, dx, dy: rc(
        E0.at[:, thinner(SRC0X[dx], dx, dy), sl(SRC0Y[dy])], E0.at[:, thinner(DST0X[dx], dx, dy), sl(DST0Y[dy])], e0s.at[n], e0r.at[n], dev_near(dx, dy)))
    c1 = near_copies(lambda n, dx, dy: rc(
        E1.at[thinner(SRC1X[dx], dx, dy), sl(SRC1Y[dy])], E1.at[thinner(DST1X[dx], dx, dy), sl(DST1Y[dy])], e1s.at[n], e1r.at[n], dev_near(dx, dy)))
    def slab_copies(first, last, base):
        return near_copies(lambda n, dx, dy: rc(
            XB.at[1, :, first:last, sl(SRC0Y[dy])], XB.at[1 - dx, :, first:last, sl(DST0Y[dy])],
            xs.at[base + n], xr.at[base + n], dev_near(dx, dy)))

    cx1, cx0 = slab_copies(2, 3, 0), slab_copies(0, 2, 8)

    gather_x = [
        rc(E23.at[gy, gx], E23.at[gy, gx], gs.at[a - 1], gr.at[a - 1], {"gx": rem(gx + a, 4)}) for a in range(1, 4)
    ]
    gather_y = []
    for b in range(1, 8):
        dev = {"gy": rem(gy + b, 8)}
        wide = rc(E23.at[gy], E23.at[gy], cs.at[b - 1], cr.at[b - 1], dev)
        thin = rc(E23.at[gy, :, 3:4], E23.at[gy, :, 3:4], cs.at[b - 1], cr.at[b - 1], dev)
        to = gy < 7 if b == 1 else gy > 0 if b == 7 else None
        of = gy > 0 if b == 1 else gy < 7 if b == 7 else None
        gather_y.append((wide, thin, to, of))

    def each_y(what, end):
        for wide, thin, to, of in gather_y:
            cond = of if end else to
            if cond is None:
                getattr(thin, what)()
            else:
                each(cond, [wide], what)
                each(jnp.logical_not(cond), [thin], what)

    for ok, _, c in c1 + [c0[1], c0[6], c0[3], c0[4], c0[0], c0[2], c0[5], c0[7]]:
        each(ok, [c], "start")

    @pl.when(gz == 0)
    def _():
        for n in range(3):
            XB[1, 0, n, 8:40] = zero32
        CB[0] = zero8

    @pl.when(gz == 7)
    def _():
        for n in range(3):
            XB[1, 1, n, 8:40] = zero32
        CB[1] = zero8

    each(gz < 7, zdown[0:1], "wait_recv")
    each(gz > 0, zup[0:1], "wait_recv")
    top = rowid(8) < 4
    E23[gy, gx, 2] = jnp.where(l8 < 64, CB[0], roll(CB[1], 64))
    E23[gy, gx, 3] = jnp.where(l8 < 64, m3, jnp.where(top, CB[0], CB[1]))
    for c in gather_x:
        c.start()
    each(gz < 7, zdown[1:3], "wait_recv")
    each(gz > 0, zup[1:3], "wait_recv")
    for ok, _, c in cx1:
        each(ok, [c], "start")

    for c in gather_x:
        c.wait_recv()
    each_y("start", False)
    each(gz < 7, zdown[3:4], "wait_recv")
    each(gz > 0, zup[3:4], "wait_recv")
    for ok, _, c in cx0:
        each(ok, [c], "start")

    for _, okr, c in c1 + cx1:
        each(okr, [c], "wait_recv")

    l32b = lanes(32)

    def load1(i):
        x = i - 7
        dx = jnp.where(x >= 0, 1, 0) + jnp.where(x >= 8, 1, 0)
        xl = x & 7
        m = mask1(i)
        main = E1[i]
        out1 = []
        lo = jnp.concatenate([XB[dx, 0, 2, 0:16], XB[dx, 0, 2, 32:48]], axis=0)
        hi = jnp.concatenate([XB[dx, 1, 2, 0:16], XB[dx, 1, 2, 32:48]], axis=0)
        for isk in range(2):
            at = 8 * xl + 64 * isk
            mid = roll(main, 64) if isk else main
            out = jnp.where(
                l32b < 64, mid,
                jnp.where(l32b < 96, roll(hi, (192 - at) & 127), roll(lo, (248 - at) & 127)),
            )
            out = jnp.where(m, out, 0.0)
            if isk:
                out1.append((L1.K, (i, slice(8, 40)), out))
            else:
                out1.append((L1.R, i, out))
        return out1

    loop(0, 22, 4, load1)
    L1.build()
    L1.smooth6()

    for _, okr, c in c0:
        each(okr, [c], "wait_recv")

    def load0(i):
        m = mask0(i)
        return [
            (L0.K, (i, slice(8, 56)), jnp.where(m, E0[1, i], 0.0)), (L0.R, i, jnp.where(m, E0[0, i], 0.0)),
        ]

    loop(0, 30, 6, load0)
    L0.build()
    L0.smooth6()

    each_y("wait_recv", True)
    in3 = yz(8, 0, 8, 16, 16, 16)
    for sx in range(4):
        def load3(q, sx=sx):
            a, b = E23[2 * q, sx, 3], E23[2 * q + 1, sx, 3]
            m = jnp.where(top, a, b)
            lo = jnp.where(top, a, pltpu.roll(b, 4, 0))
            hi = jnp.where(top, pltpu.roll(a, 4, 0), b)
            out3 = []
            for xl in range(2):
                for isk in range(2):
                    at = 32 * xl + 16 * isk
                    out = jnp.where(
                        l8 < 16, roll(m, (128 - at) % 128),
                        jnp.where(l8 < 32, roll(hi, (16 - 64 - at) % 128), roll(lo, (112 - 64 - at) % 128)),
                    )
                    out = jnp.where(in3, out, 0.0)
                    plane = 1 + 2 * sx + xl
                    if isk:
                        out3.append((L3.K, (plane, slice(8 + 8 * q, 16 + 8 * q)), out))
                    else:
                        out3.append((L3.R, (plane, slice(8 * q, 8 * q + 8)), out))
            return out3

        loop(0, 4, 4, load3)
    L3.build()
    L3.step(L3.VA, L3.VB, A1, B1, 0, True)

    def residue(i):
        _, av = L3.flux(L3.VB, i)
        return [(RES, i - 1, L3.R[i] - av)]

    loop(1, 9, 4, residue)
    in4 = mask4(0)

    def down4(x):
        t = (RES[2 * x, pl.ds(0, 16, stride=2)] + RES[2 * x, pl.ds(1, 16, stride=2)]) + (
            RES[2 * x + 1, pl.ds(0, 16, stride=2)] + RES[2 * x + 1, pl.ds(1, 16, stride=2)]
        )
        r4 = jnp.where(in4, pair(t, 16), 0.0)
        t = (L3.K[1 + 2 * x, pl.ds(8, 16, stride=2)] + L3.K[1 + 2 * x, pl.ds(9, 16, stride=2)]) + (
            L3.K[2 + 2 * x, pl.ds(8, 16, stride=2)] + L3.K[2 + 2 * x, pl.ds(9, 16, stride=2)]
        )
        k4 = jnp.where(in4, 0.125 * pair(t, 16), 0.0)
        return [(L4.R, 1 + x, r4), (L4.K, (1 + x, slice(8, 24)), k4)]

    loop(0, 4, 4, down4)
    L4.build()
    L4.step(L4.VA, L4.VB, A1, B1, 0, True)
    L4.step(L4.VB, L4.VA, A2, B2, 0)
    L4.step(L4.VA, L4.VB, A3, B3, 0)

    def repeat_lanes(x, rows):
        l = lanes(rows)
        return gat(x, jnp.where(l < 96, l >> 1, (l >> 1) + 64))

    def repeat_rows(ref, slot, x, rows):
        ref[slot, pl.ds(0, rows, stride=2)] = x
        ref[slot, pl.ds(1, rows, stride=2)] = x
        return ref[slot, 0 : 2 * rows]

    def up4(x):
        t = repeat_rows(T, x, repeat_lanes(L4.VB[1 + x, 8:24], 16), 16)
        rows = slice(8, 40)
        return [(L3.VB, (1 + 2 * x + p, rows), L3.VB[1 + 2 * x + p, rows] + t) for p in range(2)]

    loop(0, 4, 4, up4)
    L3.step(L3.VB, L3.VA, 0.0, B0, 0)
    L3.step(L3.VA, L3.VB, A1, B1, 0)

    def load2(i):
        xg = 4 * gx + i - 7 + 8
        sx = (xg >> 2) - 2
        xl = xg & 3
        scx = jnp.clip(sx, 0, 3)
        m = mask2(i)
        out2 = []
        for n in range(3):
            sy = jnp.clip(gy + n - 1, 0, 7)
            r, k, edge = E23[sy, scx, 0], E23[sy, scx, 1], E23[sy, scx, 2]
            mn = m[8 * n : 8 * n + 8]
            for isk, mid in ((0, r), (1, k)):
                at = 8 * xl + 32 * isk
                out = jnp.where(
                    l8 < 32, roll(mid, (128 - 32 * xl) & 127),
                    jnp.where(l8 < 64, roll(edge, (224 - at) & 127), roll(edge, (248 - at) & 127)),
                )
                out = jnp.where(mn, out, 0.0)
                if isk:
                    out2.append((L2.K, (i, slice(8 + 8 * n, 16 + 8 * n)), out))
                else:
                    out2.append((L2.R, (i, slice(8 * n, 8 * n + 8)), out))
        return out2

    loop(0, 18, 6, load2)
    L2.build()
    L2.smooth6()

    def up3(q):
        w = L3.VB[2 * gx + q, pl.ds(4 * gy + 4, 16)]
        t = repeat_rows(T, 4 + q, repeat_lanes(w, 16), 16)[0:24]
        rows = slice(8, 32)
        return [(L2.VB, (2 * q + 5 + p, rows), L2.VB[2 * q + 5 + p, rows] + t) for p in range(2)]

    loop(0, 4, 4, up3)

    def up2(q):
        t = repeat_rows(T, 8 + q, repeat_lanes(L2.VB[q + 6, 12:28], 16), 16)
        rows = slice(8, 40)
        return [(L1.VB, (2 * q + 5 + p, rows), L1.VB[2 * q + 5 + p, rows] + t) for p in range(2)]

    loop(0, 6, 6, up2)

    for _, okr, c in cx0:
        each(okr, [c], "wait_recv")
    ls, gsl, zz = group(48)

    def load_slab(xi):
        m = masks(xi + 1)
        x = 10 * gsl + (xi - 7)
        which = jnp.where(x >= 0, 1, 0) + jnp.where(x >= 16, 1, 0)
        xl = x & 15
        ilo = (8 * xl + zz) & 127
        ihi = (8 * xl + zz - 34) & 127
        imain = jnp.where(zz < 21, zz - 8, zz + 94) & 127
        outs = []
        for arr in range(2):
            src = L0.K if arr else L0.R
            parts = []
            for g in range(3):
                plane = src[10 * g + xi, 8:56] if arr else src[10 * g + xi]
                parts.append(gat(plane, imain))
            mid = jnp.where(gsl == 0, parts[0], jnp.where(gsl == 1, parts[1], parts[2]))
            lo = [gat(XB[d, 0, arr], ilo) for d in range(3)]
            hi = [gat(XB[d, 1, arr], ihi) for d in range(3)]
            pick = [jnp.where(which == 0, t[0], jnp.where(which == 1, t[1], t[2])) for t in (lo, hi)]
            out = jnp.where(zz < 8, pick[0], jnp.where(zz >= 34, pick[1], mid))
            out = jnp.where(m, out, 0.0)
            if arr:
                outs.append((LS.K, (1 + xi, slice(8, 56)), out))
            else:
                outs.append((LS.R, 1 + xi, out))
        return outs

    loop(0, 10, 2, load_slab)

    def ghosts(ref):
        ref[0, 8:56] = roll(ref[10, 8:56], 42)
        ref[11, 8:56] = roll(ref[1, 8:56], 86)

    ghosts(LS.K)
    LS.build()
    ghosts(LS.VA)
    LS.smooth6(after=ghosts, trim=False)

    l48, l24 = lanes(48), lanes(24)

    def merge(q):
        w = L1.VB[q + 6, 12:36]
        t = repeat_rows(T, 14 + q, gat(w, l24 >> 1), 24)
        th = repeat_rows(TH, q, gat(w, jnp.where(l24 == 0, 127, 64)), 24)
        out = []
        for p in range(2):
            i = 2 * q + 5 + p
            g = jnp.where(i >= 10, 1, 0) + jnp.where(i >= 20, 1, 0)
            xi = i - 10 * g
            sv = LS.VB[1 + xi, 8:56]
            sk = LS.K[1 + xi, 8:56]
            off = 42 * g
            v = jnp.where(
                l48 < 6, roll(sv, (248 - off) & 127),
                jnp.where(l48 >= 122, roll(sv, (222 - off) & 127), L0.VB[i, 8:56]),
            )
            hv = jnp.where(l48 < 64, roll(sv, (249 - off) & 127), roll(sv, (221 - off) & 127)) + th
            kh = jnp.where(l48 < 64, roll(sk, (249 - off) & 127), roll(sk, (221 - off) & 127))
            out += [(L0.VB, (i, slice(8, 56)), v + t), (HV, i, hv), (KH, i, kh)]
        return out

    loop(0, 10, 2, merge)

    def final(x):
        i = x + 7
        c = slice(16, 48)
        v = L0.VB[i, c]
        k = L0.K[i, c]
        hv, kh = HV[i, 8:40], KH[i, 8:40]
        out = L0.CX[i, 8:40] * (v - L0.VB[i - 1, c])
        out = out + L0.CX[i + 1, 8:40] * (v - L0.VB[i + 1, c])
        out = out + L0.CY[i, 8:40] * (v - L0.VB[i, 15:47])
        out = out + L0.CY[i, 9:41] * (v - L0.VB[i, 17:49])
        cl = 0.5 * (k + jnp.where(l32 == 0, kh, roll(k, 1)))
        cr = 0.5 * (k + jnp.where(l32 == 127, kh, roll(k, 127)))
        out = out + cl * (v - jnp.where(l32 == 0, hv, roll(v, 1)))
        out = out + cr * (v - jnp.where(l32 == 127, hv, roll(v, 127)))
        return [(corr_out, x, v), (res_out, x, E0[0, i, 8:40] - out)]

    loop(0, 16, 4, final)

    each(gz > 0, zdown, "wait_send")
    each(gz < 7, zup, "wait_send")
    for ok, _, c in c0 + c1 + cx0 + cx1:
        each(ok, [c], "wait_send")
    for c in gather_x:
        c.wait_send()
    each_y("wait_send", False)


def level_scratch(X, Y):
    big, mid = pltpu.VMEM((X, Y + 16, 128), f32), pltpu.VMEM((X, Y, 128), f32)
    return [big, mid, mid, pltpu.VMEM((X, Y + 8, 128), f32), mid, mid, mid, big, big]


def shards(source, conductivity):
    dma = pltpu.SemaphoreType.DMA
    vm = lambda *shape: pltpu.VMEM(shape, f32)
    out = jax.ShapeDtypeStruct((16, 32, 128), f32)
    scratch = [
        vm(2, 30, 48, 128), vm(22, 32, 128), vm(8, 4, 4, 8, 128), vm(3, 2, 3, 48, 128), vm(2, 3, 32, 128),
        vm(4, 8, 128), vm(2, 8, 128), vm(24, 48, 128), vm(10, 48, 128), vm(8, 32, 128), vm(30, 48, 128), vm(30, 48, 128),
        dma((2,)), dma((8,)), dma((8,)), dma((8,)), dma((8,)), dma((3,)), dma((3,)), dma((2, 4)), dma((2, 4)),
        dma((16,)), dma((16,)), dma((7,)), dma((7,)),
    ]
    for X, Y in ((30, 48), (12, 48), (22, 32), (18, 24), (10, 32), (6, 16)):
        scratch += level_scratch(X, Y)
    return pl.pallas_call(
        kernel,
        out_shape=(out, out),
        in_specs=[pl.BlockSpec(memory_space=pltpu.HBM)] * 2,
        out_specs=(pl.BlockSpec(memory_space=pltpu.VMEM),) * 2,
        scratch_shapes=scratch,
        compiler_params=pltpu.CompilerParams(
            collective_id=0, has_side_effects=True, vmem_limit_bytes=48 * 1024 * 1024
        ),
        name="multigrid",
    )(source, conductivity)


def solution(mesh):
    spec = P("gx", "gy", "gz")
    return jax.shard_map(shards, mesh=mesh, in_specs=(spec, spec), out_specs=(spec, spec), check_vma=False)
```

```python
import jax
import jax.numpy as jnp
from jax import lax
from jax.experimental import pallas as pl
from jax.experimental.pallas import tpu as pltpu
from jax.sharding import PartitionSpec as P

f32 = jnp.float32
MESH = pl.DeviceIdType.MESH

CENTRE = (2.0 + 0.3) / 2.0
HALF = (2.0 - 0.3) / 2.0
SHARP = CENTRE / HALF
W0 = 1.0 / SHARP
W1 = 1.0 / (2.0 * SHARP - W0)
W2 = 1.0 / (2.0 * SHARP - W1)
W3 = 1.0 / (2.0 * SHARP - W2)
B0 = 1.0 / CENTRE
A1, B1 = W1 * W0, 2.0 * W1 / HALF
A2, B2 = W2 * W1, 2.0 * W2 / HALF
A3, B3 = W3 * W2, 2.0 * W3 / HALF

NEAR = [(dx, dy) for dx in (-1, 0, 1) for dy in (-1, 0, 1) if (dx, dy) != (0, 0)]
DIAGONAL = [(dx, dy) for dx, dy in NEAR if dx * dy != 0]


def lanes(rows):
    return lax.broadcasted_iota(jnp.int32, (rows, 128), 1)


def rowid(rows):
    return lax.broadcasted_iota(jnp.int32, (rows, 128), 0)


def gat(x, idx):
    return jnp.take_along_axis(x, idx, axis=1, mode="promise_in_bounds")


def roll(x, shift):
    return pltpu.roll(x, shift, 1)


def loop(lo, hi, width, body):
    def chunk(first, count):
        stores = [st for u in range(count) for st in body(first + u)]
        for ref, index, value in stores:
            ref[index] = value

    def step(j, c):
        chunk(lo + j * width, width)
        return c

    whole = (hi - lo) // width
    if whole == 1:
        chunk(lo, width)
    elif whole > 1:
        lax.fori_loop(0, whole, step, 0)
    if (hi - lo) % width:
        chunk(lo + whole * width, (hi - lo) % width)


def rem(a, n):
    return lax.rem(a, n)


class Level:
    def __init__(self, refs, planes, rows, factor, mask, width):
        self.K, self.R, self.CX, self.CY, self.CZ, self.CW, self.ID, self.VA, self.VB = refs
        self.width = width
        self.X, self.Y, self.h, self.mask = planes, rows, 0.5 * factor, mask

    def clear(self):
        Y = self.Y
        pad = jnp.zeros((8, 128), f32)

        def body(i):
            out = []
            for ref in (self.K, self.VA, self.VB):
                out += [(ref, (i, slice(0, 8)), pad), (ref, (i, slice(8 + Y, 16 + Y)), pad)]
            return out

        loop(0, self.X, 6, body)
        full = jnp.zeros((Y, 128), f32)
        for i in (0, self.X - 1):
            for ref in (self.VA, self.VB, self.K):
                ref[i, 8 : 8 + Y] = full

    def build(self, start=True):
        Y, h, K = self.Y, self.h, self.K

        def body(i):
            k = K[i, 8 : 8 + Y]
            low = h * (k + K[i - 1, 8 : 8 + Y])
            high = h * (k + K[i + 1, 8 : 8 + Y])
            cy = h * (K[i, 8 : 16 + Y] + K[i, 7 : 15 + Y])
            cz = h * (k + roll(k, 1))
            cw = h * (k + roll(k, 127))
            ylow = h * (k + K[i, 7 : 7 + Y])
            yhigh = h * (k + K[i, 9 : 9 + Y])
            d = low + high + ylow + yhigh + cz + cw
            inv = jnp.where(self.mask(i), 1.0 / d, 0.0)
            first = [(self.VA, (i, slice(8, 8 + Y)), B0 * (self.R[i] * inv))] if start else []
            return first + [
                (self.CX, i, low), (self.CX, i + 1, high), (self.CY, i, cy), (self.CZ, i, cz), (self.CW, i, cw),
                (self.ID, i, inv),
            ]

        loop(1, self.X - 1, self.width, body)

    def flux(self, V, i):
        Y = self.Y
        v = V[i, 8 : 8 + Y]
        out = self.CX[i] * (v - V[i - 1, 8 : 8 + Y])
        out = out + self.CX[i + 1] * (v - V[i + 1, 8 : 8 + Y])
        out = out + self.CY[i, 0:Y] * (v - V[i, 7 : 7 + Y])
        out = out + self.CY[i, 1 : 1 + Y] * (v - V[i, 9 : 9 + Y])
        out = out + self.CZ[i] * (v - roll(v, 1))
        return v, out + self.CW[i] * (v - roll(v, 127))

    def step(self, src, dst, a, b, shrink, first=False):
        Y = self.Y

        def body(i):
            v, av = self.flux(src, i)
            new = v + b * (self.ID[i] * (self.R[i] - av))
            if first:
                new = new + a * v
            elif a != 0.0:
                new = new + a * (v - dst[i, 8 : 8 + Y])
            return [(dst, (i, slice(8, 8 + Y)), new)]

        loop(1 + shrink, self.X - 1 - shrink, self.width, body)

    def smooth6(self, after=None, trim=True):
        plan = [
            (self.VA, self.VB, A1, B1, True),
            (self.VB, self.VA, A2, B2, False),
            (self.VA, self.VB, 0.0, B0, False),
            (self.VB, self.VA, A1, B1, False),
            (self.VA, self.VB, A2, B2, False),
        ]
        for n, (src, dst, a, b, first) in enumerate(plan):
            self.step(src, dst, a, b, n + 1 if trim else 0, first)
            if after is not None and n < 4:
                after(dst)


def kernel(r_in, k_in, corr_out, res_out, *s):
    (E0, E1, E23, XB, PB, RK2, CB, T, TH, RES, HV, KH, sem_loc, e0s, e0r, e1s, e1r, gs, gr, bs, br, xs, xr, cs, cr, *lv) = s
    gx, gy, gz = lax.axis_index("gx"), lax.axis_index("gy"), lax.axis_index("gz")

    loc = [
        pltpu.make_async_copy(ref, E0.at[n, 7:23, 8:40], sem_loc.at[n]) for n, ref in enumerate((r_in, k_in))
    ]
    for c in loc:
        c.start()

    bar = pltpu.get_barrier_semaphore()

    def inside(dx, dy):
        return (gx + dx >= 0) & (gx + dx < 4) & (gy + dy >= 0) & (gy + dy < 8)

    def greet(dev):
        pl.semaphore_signal(bar, inc=1, device_id=dev, device_id_type=MESH)

    @pl.when(gz > 0)
    def _():
        greet({"gz": gz - 1})

    @pl.when(gz < 7)
    def _():
        greet({"gz": gz + 1})

    for a in range(1, 4):
        greet({"gx": rem(gx + a, 4)})
    for b in range(1, 8):
        greet({"gy": rem(gy + b, 8)})
    for dx, dy in DIAGONAL:
        pl.when(inside(dx, dy))(lambda dx=dx, dy=dy: greet({"gx": gx + dx, "gy": gy + dy}))

    def yz(rows, ylo, ny, zlo, zown, zhi):
        y = rowid(rows) + ylo
        l = lanes(rows)
        low = jnp.where(gz > 0, 128 - zlo, 128)
        high = jnp.where(gz < 7, zown + zhi, zown)
        return (y >= 0) & (y < ny) & ((l < high) | (l >= low))

    def with_x(base, rows, x, nx):
        xv = jnp.zeros((rows, 128), jnp.int32) + x
        return base & (xv >= 0) & (xv < nx)

    def mask0(i):
        return with_x(yz(48, 32 * gy - 8, 256, 0, 128, 0), 48, 16 * gx + i - 7, 64)

    def group(rows):
        l = lanes(rows)
        g = jnp.where(l >= 84, 2, jnp.where(l >= 42, 1, 0))
        return l, g, l - 42 * g

    def masks(i):
        l, g, zz = group(48)
        y = rowid(48) + (32 * gy - 8)
        x = 10 * g + (16 * gx + i - 8)
        low = jnp.where(gz > 0, 0, 8)
        high = jnp.where(gz < 7, 42, 34)
        return (y >= 0) & (y < 256) & (x >= 0) & (x < 64) & (zz >= low) & (zz < high) & (l < 126)

    def mask1(i):
        return with_x(yz(32, 16 * gy - 8, 128, 8, 64, 8), 32, 8 * gx + i - 7, 32)

    def mask2(i):
        return with_x(yz(24, 8 * gy - 8, 64, 8, 32, 8), 24, 4 * gx + i - 7, 16)

    def mask3(i):
        return yz(32, 0, 32, 16, 16, 16)

    def mask4(i):
        return yz(16, 0, 16, 8, 8, 8)

    L0 = Level(lv[0:9], 30, 48, 1.0, mask0, 8)
    LS = Level(lv[9:18], 12, 48, 1.0, masks, 10)
    L1 = Level(lv[18:27], 22, 32, 2.0, mask1, 10)
    L2 = Level(lv[27:36], 18, 24, 4.0, mask2, 8)
    L3 = Level(lv[36:45], 10, 32, 8.0, mask3, 8)
    L4 = Level(lv[45:54], 6, 16, 16.0, mask4, 4)

    for c in loc:
        c.wait()

    l32 = lanes(32)
    zero32 = jnp.zeros((32, 128), f32)

    def pack0(x, c):
        r8, k8 = (roll(E0[n, 7 + x, 8:40], 8 * x) for n in range(2))
        here, before = (l32 >> 3) == x, (l32 >> 3) == ((x + 15) & 15)
        return (
            jnp.where(here, r8, c[0]),
            jnp.where(here, k8, c[1]),
            jnp.where(before, r8, c[2]),
            jnp.where(before, k8, c[3]),
        )

    packed = (zero32,) * 4
    for x in range(16):
        packed = pack0(x, packed)
    PB[0, 0], PB[0, 1] = packed[0], packed[1]
    PB[1, 0], PB[1, 1] = roll(packed[2], 8), roll(packed[3], 8)

    def pair(x, rows):
        l = lanes(rows)
        return gat(x, (2 * l) & 127) + gat(x, (2 * l + 1) & 127)

    l16 = lanes(16)

    def down1(x, c):
        out = []
        for n in range(2):
            a, b = (E0[n, 7 + 2 * x + p, pl.ds(8, 16, stride=2)] + E0[n, 7 + 2 * x + p, pl.ds(9, 16, stride=2)] for p in range(2))
            t = a + b
            out.append(pair(t, 16))
        rk = jnp.where(l16 < 64, out[0], 0.125 * out[1])
        E1[7 + x, 8:24] = rk
        here = ((l16 & 63) >> 3) == x
        return (
            jnp.where(here, roll(rk, 8 * x), c[0]),
            jnp.where(here, roll(rk, (8 * x + 72) & 127), c[1]),
        )

    zero16 = jnp.zeros((16, 128), f32)
    low1 = high1 = zero16
    for x in range(8):
        low1, high1 = down1(x, (low1, high1))
    for side, val in enumerate((low1, high1)):
        PB[side, 2, 0:8] = val[0:8]
        PB[side, 2, 24:32] = val[8:16]

    l8 = lanes(8)
    zero8 = jnp.zeros((8, 128), f32)

    def down2(x, c):
        def part(p, n):
            return E1[7 + 2 * x + p, pl.ds(8 + n, 8, stride=2)]

        t = (part(0, 0) + part(0, 1)) + (part(1, 0) + part(1, 1))
        rk = pair(t, 8)
        rk = jnp.where(((l8 >> 5) & 1) == 1, 0.125 * rk, rk)
        RK2[x] = rk
        here, edge = (l8 >> 5) == x, (l8 < 64) & (((l8 & 31) >> 3) == x)
        return (
            jnp.where(here, roll(rk, 32 * x), c[0]),
            jnp.where(here, roll(rk, (32 * x + 96) & 127), c[1]),
            jnp.where(edge, roll(rk, 8 * x), c[2]),
            jnp.where(edge, roll(rk, (8 * x + 104) & 127), c[3]),
        )

    r2 = k2 = low2 = high2 = zero8
    for x in range(4):
        r2, k2, low2, high2 = down2(x, (r2, k2, low2, high2))
    l4 = lanes(4)
    rk3 = []
    for x in range(2):
        t = (RK2[2 * x, pl.ds(0, 4, stride=2)] + RK2[2 * x, pl.ds(1, 4, stride=2)]) + (
            RK2[2 * x + 1, pl.ds(0, 4, stride=2)] + RK2[2 * x + 1, pl.ds(1, 4, stride=2)]
        )
        T[x, 0:4], T[x, 4:8] = t, t
        t = pair(T[x, 0:8], 8)
        rk3.append(jnp.where(((l8 >> 4) & 1) == 1, 0.125 * t, t))
    m3 = jnp.where(((l8 >> 5) & 1) == 0, rk3[0], rk3[1])
    E23[gy, gx, 0], E23[gy, gx, 1] = r2, k2
    RK2[0] = jnp.where(l8 < 64, low2, m3)
    RK2[1] = jnp.where(l8 < 64, high2, m3)

    for L in (L0, LS, L1, L2, L3, L4):
        L.clear()

    def sides(at, n):
        return jnp.where(at > 0, 1, 0) + jnp.where(at < n - 1, 1, 0)

    pl.semaphore_wait(bar, 10 + sides(gx, 4) * sides(gy, 8) + sides(gz, 8))

    def zcopies(side):
        dev = {"gz": gz - 1 if side == 0 else gz + 1}
        land = 1 - side
        pieces = [
            (RK2.at[side], CB.at[land]),
            (PB.at[side, 2, 0:8], XB.at[1, land, 2, 8:16]),
            (PB.at[side, 2, 24:32], XB.at[1, land, 2, 32:40]),
            (PB.at[side, 0:2], XB.at[1, land, 0:2, 8:40]),
        ]
        return [
            pltpu.make_async_remote_copy(
                src_ref=src, dst_ref=dst, send_sem=bs.at[side, n], recv_sem=br.at[side, n],
                device_id=dev, device_id_type=MESH,
            )
            for n, (src, dst) in enumerate(pieces)
        ]

    def each(cond, copies, what):
        @pl.when(cond)
        def _():
            for c in copies:
                getattr(c, what)()

    zdown, zup = zcopies(0), zcopies(1)
    each(gz > 0, zdown, "start")
    each(gz < 7, zup, "start")

    SRC0X, DST0X = {-1: (7, 14), 0: (7, 23), 1: (16, 23)}, {-1: (23, 30), 0: (7, 23), 1: (0, 7)}
    SRC0Y, DST0Y = {-1: (8, 16), 0: (8, 40), 1: (32, 40)}, {-1: (40, 48), 0: (8, 40), 1: (0, 8)}
    SRC1X, DST1X = {-1: (7, 14), 0: (7, 15), 1: (8, 15)}, {-1: (15, 22), 0: (7, 15), 1: (0, 7)}
    SRC1Y, DST1Y = {-1: (8, 16), 0: (8, 24), 1: (16, 24)}, {-1: (24, 32), 0: (8, 24), 1: (0, 8)}

    def sl(pairs):
        return pl.ds(pairs[0], pairs[1] - pairs[0])

    def near_copies(make):
        return [(inside(dx, dy), inside(-dx, -dy), make(n, dx, dy)) for n, (dx, dy) in enumerate(NEAR)]

    def rc(src, dst, ss, rs, dev):
        return pltpu.make_async_remote_copy(
            src_ref=src, dst_ref=dst, send_sem=ss, recv_sem=rs, device_id=dev, device_id_type=MESH
        )

    def dev_near(dx, dy):
        return {"gx": gx + dx, "gy": gy + dy}

    def thinner(pairs, dx, dy):
        if dx == 0 or dy == 0:
            return sl(pairs)
        return sl((pairs[0] + 1, pairs[1])) if dx == 1 else sl((pairs[0], pairs[1] - 1))

    def fine(arr):
        return near_copies(lambda n, dx, dy: rc(
            E0.at[arr, thinner(SRC0X[dx], dx, dy), sl(SRC0Y[dy])], E0.at[arr, thinner(DST0X[dx], dx, dy), sl(DST0Y[dy])],
            e0s.at[8 * arr + n], e0r.at[8 * arr + n], dev_near(dx, dy)))

    c0r, c0k = fine(0), fine(1)
    c1 = near_copies(lambda n, dx, dy: rc(
        E1.at[thinner(SRC1X[dx], dx, dy), sl(SRC1Y[dy])], E1.at[thinner(DST1X[dx], dx, dy), sl(DST1Y[dy])], e1s.at[n], e1r.at[n], dev_near(dx, dy)))
    def slab_copies(first, last, base):
        return near_copies(lambda n, dx, dy: rc(
            XB.at[1, :, first:last, sl(SRC0Y[dy])], XB.at[1 - dx, :, first:last, sl(DST0Y[dy])],
            xs.at[base + n], xr.at[base + n], dev_near(dx, dy)))

    cx1, cx0 = slab_copies(2, 3, 0), slab_copies(0, 2, 8)

    gather_x = [
        rc(E23.at[gy, gx], E23.at[gy, gx], gs.at[a - 1], gr.at[a - 1], {"gx": rem(gx + a, 4)}) for a in range(1, 4)
    ]
    gather_y = []
    for b in range(1, 8):
        dev = {"gy": rem(gy + b, 8)}
        wide = rc(E23.at[gy], E23.at[gy], cs.at[b - 1], cr.at[b - 1], dev)
        thin = rc(E23.at[gy, :, 3:4], E23.at[gy, :, 3:4], cs.at[b - 1], cr.at[b - 1], dev)
        up, fromlow = gy + b < 8, gy - b >= 0
        if b == 4:
            gather_y.append((thin, None, None))
        elif b < 4:
            gather_y.append((wide if b == 1 else thin, up, fromlow))
        else:
            gather_y.append((wide if b == 7 else thin, jnp.logical_not(up), jnp.logical_not(fromlow)))

    def each_y(what, end):
        for copy, to, of in gather_y:
            cond = of if end else to
            if cond is None:
                getattr(copy, what)()
            else:
                each(cond, [copy], what)

    for ok, _, c in c1 + [c0k[n] for n in (1, 6, 3, 4, 0, 2, 5, 7)]:
        each(ok, [c], "start")

    @pl.when(gz == 0)
    def _():
        for n in range(3):
            XB[1, 0, n, 8:40] = zero32
        CB[0] = zero8

    @pl.when(gz == 7)
    def _():
        for n in range(3):
            XB[1, 1, n, 8:40] = zero32
        CB[1] = zero8

    each(gz < 7, zdown[0:1], "wait_recv")
    each(gz > 0, zup[0:1], "wait_recv")
    top = rowid(8) < 4
    E23[gy, gx, 2] = jnp.where(l8 < 64, CB[0], roll(CB[1], 64))
    E23[gy, gx, 3] = jnp.where(l8 < 64, m3, jnp.where(top, CB[0], CB[1]))
    for c in gather_x:
        c.start()
    each(gz < 7, zdown[1:3], "wait_recv")
    each(gz > 0, zup[1:3], "wait_recv")
    for ok, _, c in cx1 + [c0r[n] for n in (1, 6, 3, 4, 0, 2, 5, 7)]:
        each(ok, [c], "start")

    for c in gather_x:
        c.wait_recv()
    each_y("start", False)
    each(gz < 7, zdown[3:4], "wait_recv")
    each(gz > 0, zup[3:4], "wait_recv")
    for ok, _, c in cx0:
        each(ok, [c], "start")

    for _, okr, c in c1 + cx1:
        each(okr, [c], "wait_recv")

    l32b = lanes(32)

    def load1(i):
        x = i - 7
        dx = jnp.where(x >= 0, 1, 0) + jnp.where(x >= 8, 1, 0)
        xl = x & 7
        m = mask1(i)
        main = E1[i]
        out1 = []
        lo = jnp.concatenate([XB[dx, 0, 2, 0:16], XB[dx, 0, 2, 32:48]], axis=0)
        hi = jnp.concatenate([XB[dx, 1, 2, 0:16], XB[dx, 1, 2, 32:48]], axis=0)
        for isk in range(2):
            at = 8 * xl + 64 * isk
            mid = roll(main, 64) if isk else main
            out = jnp.where(
                l32b < 64, mid,
                jnp.where(l32b < 96, roll(hi, (192 - at) & 127), roll(lo, (248 - at) & 127)),
            )
            out = jnp.where(m, out, 0.0)
            if isk:
                out1.append((L1.K, (i, slice(8, 40)), out))
            else:
                out1.append((L1.R, i, out))
        return out1

    loop(0, 22, 4, load1)
    L1.build()
    L1.smooth6()

    for _, okr, c in c0k:
        each(okr, [c], "wait_recv")
    loop(0, 30, 6, lambda i: [(L0.K, (i, slice(8, 56)), jnp.where(mask0(i), E0[1, i], 0.0))])
    L0.build(start=False)
    for _, okr, c in c0r:
        each(okr, [c], "wait_recv")

    def load0(i):
        r = jnp.where(mask0(i), E0[0, i], 0.0)
        return [(L0.R, i, r), (L0.VA, (i, slice(8, 56)), B0 * (r * L0.ID[i]))]

    loop(1, 29, 7, load0)
    L0.smooth6()

    for _, okr, c in cx0:
        each(okr, [c], "wait_recv")
    ls, gsl, zz = group(48)

    def load_slab(xi):
        m = masks(xi + 1)
        x = 10 * gsl + (xi - 7)
        which = jnp.where(x >= 0, 1, 0) + jnp.where(x >= 16, 1, 0)
        xl = x & 15
        ilo = (8 * xl + zz) & 127
        ihi = (8 * xl + zz - 34) & 127
        imain = jnp.where(zz < 21, zz - 8, zz + 94) & 127
        outs = []
        for arr in range(2):
            src = L0.K if arr else L0.R
            parts = []
            for g in range(3):
                plane = src[10 * g + xi, 8:56] if arr else src[10 * g + xi]
                parts.append(gat(plane, imain))
            mid = jnp.where(gsl == 0, parts[0], jnp.where(gsl == 1, parts[1], parts[2]))
            lo = [gat(XB[d, 0, arr], ilo) for d in range(3)]
            hi = [gat(XB[d, 1, arr], ihi) for d in range(3)]
            pick = [jnp.where(which == 0, t[0], jnp.where(which == 1, t[1], t[2])) for t in (lo, hi)]
            out = jnp.where(zz < 8, pick[0], jnp.where(zz >= 34, pick[1], mid))
            out = jnp.where(m, out, 0.0)
            if arr:
                outs.append((LS.K, (1 + xi, slice(8, 56)), out))
            else:
                outs.append((LS.R, 1 + xi, out))
        return outs

    loop(0, 10, 2, load_slab)

    def ghosts(ref):
        ref[0, 8:56] = roll(ref[10, 8:56], 42)
        ref[11, 8:56] = roll(ref[1, 8:56], 86)

    ghosts(LS.K)
    LS.build()
    ghosts(LS.VA)
    LS.smooth6(after=ghosts, trim=False)

    each_y("wait_recv", True)
    in3 = yz(8, 0, 8, 16, 16, 16)
    for sx in range(4):
        def load3(q, sx=sx):
            a, b = E23[2 * q, sx, 3], E23[2 * q + 1, sx, 3]
            m = jnp.where(top, a, b)
            lo = jnp.where(top, a, pltpu.roll(b, 4, 0))
            hi = jnp.where(top, pltpu.roll(a, 4, 0), b)
            out3 = []
            for xl in range(2):
                for isk in range(2):
                    at = 32 * xl + 16 * isk
                    out = jnp.where(
                        l8 < 16, roll(m, (128 - at) % 128),
                        jnp.where(l8 < 32, roll(hi, (16 - 64 - at) % 128), roll(lo, (112 - 64 - at) % 128)),
                    )
                    out = jnp.where(in3, out, 0.0)
                    plane = 1 + 2 * sx + xl
                    if isk:
                        out3.append((L3.K, (plane, slice(8 + 8 * q, 16 + 8 * q)), out))
                    else:
                        out3.append((L3.R, (plane, slice(8 * q, 8 * q + 8)), out))
            return out3

        loop(0, 4, 4, load3)
    L3.build()
    L3.step(L3.VA, L3.VB, A1, B1, 0, True)

    def residue(i):
        _, av = L3.flux(L3.VB, i)
        return [(RES, i - 1, L3.R[i] - av)]

    loop(1, 9, 4, residue)
    in4 = mask4(0)

    def down4(x):
        t = (RES[2 * x, pl.ds(0, 16, stride=2)] + RES[2 * x, pl.ds(1, 16, stride=2)]) + (
            RES[2 * x + 1, pl.ds(0, 16, stride=2)] + RES[2 * x + 1, pl.ds(1, 16, stride=2)]
        )
        r4 = jnp.where(in4, pair(t, 16), 0.0)
        t = (L3.K[1 + 2 * x, pl.ds(8, 16, stride=2)] + L3.K[1 + 2 * x, pl.ds(9, 16, stride=2)]) + (
            L3.K[2 + 2 * x, pl.ds(8, 16, stride=2)] + L3.K[2 + 2 * x, pl.ds(9, 16, stride=2)]
        )
        k4 = jnp.where(in4, 0.125 * pair(t, 16), 0.0)
        return [(L4.R, 1 + x, r4), (L4.K, (1 + x, slice(8, 24)), k4)]

    loop(0, 4, 4, down4)
    L4.build()
    L4.step(L4.VA, L4.VB, A1, B1, 0, True)
    L4.step(L4.VB, L4.VA, A2, B2, 0)
    L4.step(L4.VA, L4.VB, A3, B3, 0)

    def repeat_lanes(x, rows):
        l = lanes(rows)
        return gat(x, jnp.where(l < 96, l >> 1, (l >> 1) + 64))

    def repeat_rows(ref, slot, x, rows):
        ref[slot, pl.ds(0, rows, stride=2)] = x
        ref[slot, pl.ds(1, rows, stride=2)] = x
        return ref[slot, 0 : 2 * rows]

    def up4(x):
        t = repeat_rows(T, x, repeat_lanes(L4.VB[1 + x, 8:24], 16), 16)
        rows = slice(8, 40)
        return [(L3.VB, (1 + 2 * x + p, rows), L3.VB[1 + 2 * x + p, rows] + t) for p in range(2)]

    loop(0, 4, 4, up4)
    L3.step(L3.VB, L3.VA, 0.0, B0, 0)
    L3.step(L3.VA, L3.VB, A1, B1, 0)

    def load2(i):
        xg = 4 * gx + i - 7 + 8
        sx = (xg >> 2) - 2
        xl = xg & 3
        scx = jnp.clip(sx, 0, 3)
        m = mask2(i)
        out2 = []
        for n in range(3):
            sy = jnp.clip(gy + n - 1, 0, 7)
            r, k, edge = E23[sy, scx, 0], E23[sy, scx, 1], E23[sy, scx, 2]
            mn = m[8 * n : 8 * n + 8]
            for isk, mid in ((0, r), (1, k)):
                at = 8 * xl + 32 * isk
                out = jnp.where(
                    l8 < 32, roll(mid, (128 - 32 * xl) & 127),
                    jnp.where(l8 < 64, roll(edge, (224 - at) & 127), roll(edge, (248 - at) & 127)),
                )
                out = jnp.where(mn, out, 0.0)
                if isk:
                    out2.append((L2.K, (i, slice(8 + 8 * n, 16 + 8 * n)), out))
                else:
                    out2.append((L2.R, (i, slice(8 * n, 8 * n + 8)), out))
        return out2

    loop(0, 18, 6, load2)
    L2.build()
    L2.smooth6()

    def up3(q):
        w = L3.VB[2 * gx + q, pl.ds(4 * gy + 4, 16)]
        t = repeat_rows(T, 4 + q, repeat_lanes(w, 16), 16)[0:24]
        rows = slice(8, 32)
        return [(L2.VB, (2 * q + 5 + p, rows), L2.VB[2 * q + 5 + p, rows] + t) for p in range(2)]

    loop(0, 4, 4, up3)

    def up2(q):
        t = repeat_rows(T, 8 + q, repeat_lanes(L2.VB[q + 6, 12:28], 16), 16)
        rows = slice(8, 40)
        return [(L1.VB, (2 * q + 5 + p, rows), L1.VB[2 * q + 5 + p, rows] + t) for p in range(2)]

    loop(0, 6, 6, up2)

    l48, l24 = lanes(48), lanes(24)

    def merge(q):
        w = L1.VB[q + 6, 12:36]
        t = repeat_rows(T, 14 + q, gat(w, l24 >> 1), 24)
        th = repeat_rows(TH, q, gat(w, jnp.where(l24 == 0, 127, 64)), 24)
        out = []
        for p in range(2):
            i = 2 * q + 5 + p
            g = jnp.where(i >= 10, 1, 0) + jnp.where(i >= 20, 1, 0)
            xi = i - 10 * g
            sv = LS.VB[1 + xi, 8:56]
            sk = LS.K[1 + xi, 8:56]
            off = 42 * g
            v = jnp.where(
                l48 < 6, roll(sv, (248 - off) & 127),
                jnp.where(l48 >= 122, roll(sv, (222 - off) & 127), L0.VB[i, 8:56]),
            )
            hv = jnp.where(l48 < 64, roll(sv, (249 - off) & 127), roll(sv, (221 - off) & 127)) + th
            kh = jnp.where(l48 < 64, roll(sk, (249 - off) & 127), roll(sk, (221 - off) & 127))
            out += [(L0.VB, (i, slice(8, 56)), v + t), (HV, i, hv), (KH, i, kh)]
        return out

    loop(0, 10, 2, merge)

    def final(x):
        i = x + 7
        c = slice(16, 48)
        v = L0.VB[i, c]
        k = L0.K[i, c]
        hv, kh = HV[i, 8:40], KH[i, 8:40]
        out = L0.CX[i, 8:40] * (v - L0.VB[i - 1, c])
        out = out + L0.CX[i + 1, 8:40] * (v - L0.VB[i + 1, c])
        out = out + L0.CY[i, 8:40] * (v - L0.VB[i, 15:47])
        out = out + L0.CY[i, 9:41] * (v - L0.VB[i, 17:49])
        cl = 0.5 * (k + jnp.where(l32 == 0, kh, roll(k, 1)))
        cr = 0.5 * (k + jnp.where(l32 == 127, kh, roll(k, 127)))
        out = out + cl * (v - jnp.where(l32 == 0, hv, roll(v, 1)))
        out = out + cr * (v - jnp.where(l32 == 127, hv, roll(v, 127)))
        return [(corr_out, x, v), (res_out, x, E0[0, i, 8:40] - out)]

    loop(0, 16, 4, final)

    each(gz > 0, zdown, "wait_send")
    each(gz < 7, zup, "wait_send")
    for ok, _, c in c0r + c0k + c1 + cx0 + cx1:
        each(ok, [c], "wait_send")
    for c in gather_x:
        c.wait_send()
    each_y("wait_send", False)


def level_scratch(X, Y):
    big, mid = pltpu.VMEM((X, Y + 16, 128), f32), pltpu.VMEM((X, Y, 128), f32)
    return [big, mid, mid, pltpu.VMEM((X, Y + 8, 128), f32), mid, mid, mid, big, big]


def shards(source, conductivity):
    dma = pltpu.SemaphoreType.DMA
    vm = lambda *shape: pltpu.VMEM(shape, f32)
    out = jax.ShapeDtypeStruct((16, 32, 128), f32)
    scratch = [
        vm(2, 30, 48, 128), vm(22, 32, 128), vm(8, 4, 4, 8, 128), vm(3, 2, 3, 48, 128), vm(2, 3, 32, 128),
        vm(4, 8, 128), vm(2, 8, 128), vm(24, 48, 128), vm(10, 48, 128), vm(8, 32, 128), vm(30, 48, 128), vm(30, 48, 128),
        dma((2,)), dma((16,)), dma((16,)), dma((8,)), dma((8,)), dma((3,)), dma((3,)), dma((2, 4)), dma((2, 4)),
        dma((16,)), dma((16,)), dma((7,)), dma((7,)),
    ]
    for X, Y in ((30, 48), (12, 48), (22, 32), (18, 24), (10, 32), (6, 16)):
        scratch += level_scratch(X, Y)
    return pl.pallas_call(
        kernel,
        out_shape=(out, out),
        in_specs=[pl.BlockSpec(memory_space=pltpu.HBM)] * 2,
        out_specs=(pl.BlockSpec(memory_space=pltpu.VMEM),) * 2,
        scratch_shapes=scratch,
        compiler_params=pltpu.CompilerParams(
            collective_id=0, has_side_effects=True, vmem_limit_bytes=48 * 1024 * 1024
        ),
        name="multigrid",
    )(source, conductivity)


def solution(mesh):
    spec = P("gx", "gy", "gz")
    return jax.shard_map(shards, mesh=mesh, in_specs=(spec, spec), out_specs=(spec, spec), check_vma=False)
```

```python
import jax
import jax.numpy as jnp
from jax import lax
from jax.experimental import pallas as pl
from jax.experimental.pallas import tpu as pltpu
from jax.sharding import PartitionSpec as P

f32 = jnp.float32
MESH = pl.DeviceIdType.MESH

CENTRE = (2.0 + 0.3) / 2.0
HALF = (2.0 - 0.3) / 2.0
SHARP = CENTRE / HALF
W0 = 1.0 / SHARP
W1 = 1.0 / (2.0 * SHARP - W0)
W2 = 1.0 / (2.0 * SHARP - W1)
W3 = 1.0 / (2.0 * SHARP - W2)
B0 = 1.0 / CENTRE
A1, B1 = W1 * W0, 2.0 * W1 / HALF
A2, B2 = W2 * W1, 2.0 * W2 / HALF
A3, B3 = W3 * W2, 2.0 * W3 / HALF

NEAR = [(dx, dy) for dx in (-1, 0, 1) for dy in (-1, 0, 1) if (dx, dy) != (0, 0)]
DIAGONAL = [(dx, dy) for dx, dy in NEAR if dx * dy != 0]


def lanes(rows):
    return lax.broadcasted_iota(jnp.int32, (rows, 128), 1)


def rowid(rows):
    return lax.broadcasted_iota(jnp.int32, (rows, 128), 0)


def gat(x, idx):
    return jnp.take_along_axis(x, idx, axis=1, mode="promise_in_bounds")


def roll(x, shift):
    return pltpu.roll(x, shift, 1)


def loop(lo, hi, width, body):
    def chunk(first, count):
        stores = [st for u in range(count) for st in body(first + u)]
        for ref, index, value in stores:
            ref[index] = value

    def step(j, c):
        chunk(lo + j * width, width)
        return c

    whole = (hi - lo) // width
    if whole == 1:
        chunk(lo, width)
    elif whole > 1:
        lax.fori_loop(0, whole, step, 0)
    if (hi - lo) % width:
        chunk(lo + whole * width, (hi - lo) % width)


def rem(a, n):
    return lax.rem(a, n)


class Level:
    def __init__(self, refs, planes, rows, factor, mask, width):
        self.K, self.R, self.CX, self.CY, self.CZ, self.CW, self.ID, self.VA, self.VB = refs
        self.width = width
        self.X, self.Y, self.h, self.mask = planes, rows, 0.5 * factor, mask

    def clear(self):
        Y = self.Y
        pad = jnp.zeros((8, 128), f32)

        def body(i):
            out = []
            for ref in (self.K, self.VA, self.VB):
                out += [(ref, (i, slice(0, 8)), pad), (ref, (i, slice(8 + Y, 16 + Y)), pad)]
            return out

        loop(0, self.X, 6, body)
        full = jnp.zeros((Y, 128), f32)
        for i in (0, self.X - 1):
            for ref in (self.VA, self.VB, self.K):
                ref[i, 8 : 8 + Y] = full

    def build(self, start=True):
        Y, h, K = self.Y, self.h, self.K

        def body(i):
            k = K[i, 8 : 8 + Y]
            low = h * (k + K[i - 1, 8 : 8 + Y])
            high = h * (k + K[i + 1, 8 : 8 + Y])
            cy = h * (K[i, 8 : 16 + Y] + K[i, 7 : 15 + Y])
            cz = h * (k + roll(k, 1))
            cw = h * (k + roll(k, 127))
            ylow = h * (k + K[i, 7 : 7 + Y])
            yhigh = h * (k + K[i, 9 : 9 + Y])
            d = low + high + ylow + yhigh + cz + cw
            inv = jnp.where(self.mask(i), 1.0 / d, 0.0)
            first = [(self.VA, (i, slice(8, 8 + Y)), B0 * (self.R[i] * inv))] if start else []
            return first + [
                (self.CX, i, low), (self.CX, i + 1, high), (self.CY, i, cy), (self.CZ, i, cz), (self.CW, i, cw),
                (self.ID, i, inv),
            ]

        loop(1, self.X - 1, self.width, body)

    def flux(self, V, i):
        Y = self.Y
        v = V[i, 8 : 8 + Y]
        out = self.CX[i] * (v - V[i - 1, 8 : 8 + Y])
        out = out + self.CX[i + 1] * (v - V[i + 1, 8 : 8 + Y])
        out = out + self.CY[i, 0:Y] * (v - V[i, 7 : 7 + Y])
        out = out + self.CY[i, 1 : 1 + Y] * (v - V[i, 9 : 9 + Y])
        out = out + self.CZ[i] * (v - roll(v, 1))
        return v, out + self.CW[i] * (v - roll(v, 127))

    def step(self, src, dst, a, b, shrink, first=False):
        Y = self.Y

        def body(i):
            v, av = self.flux(src, i)
            new = v + b * (self.ID[i] * (self.R[i] - av))
            if first:
                new = new + a * v
            elif a != 0.0:
                new = new + a * (v - dst[i, 8 : 8 + Y])
            return [(dst, (i, slice(8, 8 + Y)), new)]

        loop(1 + shrink, self.X - 1 - shrink, self.width, body)

    def smooth6(self, after=None, trim=True):
        plan = [
            (self.VA, self.VB, A1, B1, True),
            (self.VB, self.VA, A2, B2, False),
            (self.VA, self.VB, 0.0, B0, False),
            (self.VB, self.VA, A1, B1, False),
            (self.VA, self.VB, A2, B2, False),
        ]
        for n, (src, dst, a, b, first) in enumerate(plan):
            self.step(src, dst, a, b, n + 1 if trim else 0, first)
            if after is not None and n < 4:
                after(dst)


def kernel(r_in, k_in, corr_out, res_out, *s):
    (E0, E1, E23, XB, PB, RK2, CB, T, TH, RES, HV, KH, sem_loc, e0s, e0r, e1s, e1r, gs, gr, bs, br, xs, xr, cs, cr, *lv) = s
    gx, gy, gz = lax.axis_index("gx"), lax.axis_index("gy"), lax.axis_index("gz")

    loc = [
        pltpu.make_async_copy(ref, E0.at[n, 7:23, 8:40], sem_loc.at[n]) for n, ref in enumerate((r_in, k_in))
    ]
    for c in loc:
        c.start()

    bar = pltpu.get_barrier_semaphore()

    def inside(dx, dy):
        return (gx + dx >= 0) & (gx + dx < 4) & (gy + dy >= 0) & (gy + dy < 8)

    def greet(dev):
        pl.semaphore_signal(bar, inc=1, device_id=dev, device_id_type=MESH)

    @pl.when(gz > 0)
    def _():
        greet({"gz": gz - 1})

    @pl.when(gz < 7)
    def _():
        greet({"gz": gz + 1})

    for a in range(1, 4):
        greet({"gx": rem(gx + a, 4)})
    for b in range(1, 8):
        greet({"gy": rem(gy + b, 8)})
    for dx, dy in DIAGONAL:
        pl.when(inside(dx, dy))(lambda dx=dx, dy=dy: greet({"gx": gx + dx, "gy": gy + dy}))

    def yz(rows, ylo, ny, zlo, zown, zhi):
        y = rowid(rows) + ylo
        l = lanes(rows)
        low = jnp.where(gz > 0, 128 - zlo, 128)
        high = jnp.where(gz < 7, zown + zhi, zown)
        return (y >= 0) & (y < ny) & ((l < high) | (l >= low))

    def with_x(base, rows, x, nx):
        xv = jnp.zeros((rows, 128), jnp.int32) + x
        return base & (xv >= 0) & (xv < nx)

    def mask0(i):
        return with_x(yz(48, 32 * gy - 8, 256, 0, 128, 0), 48, 16 * gx + i - 7, 64)

    def group(rows):
        l = lanes(rows)
        g = jnp.where(l >= 84, 2, jnp.where(l >= 42, 1, 0))
        return l, g, l - 42 * g

    def masks(i):
        l, g, zz = group(48)
        y = rowid(48) + (32 * gy - 8)
        x = 10 * g + (16 * gx + i - 8)
        low = jnp.where(gz > 0, 0, 8)
        high = jnp.where(gz < 7, 42, 34)
        return (y >= 0) & (y < 256) & (x >= 0) & (x < 64) & (zz >= low) & (zz < high) & (l < 126)

    def mask1(i):
        return with_x(yz(32, 16 * gy - 8, 128, 8, 64, 8), 32, 8 * gx + i - 7, 32)

    def mask2(i):
        return with_x(yz(24, 8 * gy - 8, 64, 8, 32, 8), 24, 4 * gx + i - 7, 16)

    def mask3(i):
        return yz(32, 0, 32, 16, 16, 16)

    def mask4(i):
        return yz(16, 0, 16, 8, 8, 8)

    L0 = Level(lv[0:9], 30, 48, 1.0, mask0, 8)
    LS = Level(lv[9:18], 12, 48, 1.0, masks, 10)
    L1 = Level(lv[18:27], 22, 32, 2.0, mask1, 10)
    L2 = Level(lv[27:36], 18, 24, 4.0, mask2, 8)
    L3 = Level(lv[36:45], 10, 32, 8.0, mask3, 8)
    L4 = Level(lv[45:54], 6, 16, 16.0, mask4, 4)

    for c in loc:
        c.wait()

    l32 = lanes(32)
    zero32 = jnp.zeros((32, 128), f32)

    def pack0(x, c):
        r8, k8 = (roll(E0[n, 7 + x, 8:40], 8 * x) for n in range(2))
        here, before = (l32 >> 3) == x, (l32 >> 3) == ((x + 15) & 15)
        return (
            jnp.where(here, r8, c[0]),
            jnp.where(here, k8, c[1]),
            jnp.where(before, r8, c[2]),
            jnp.where(before, k8, c[3]),
        )

    packed = (zero32,) * 4
    for x in range(16):
        packed = pack0(x, packed)
    PB[0, 0], PB[0, 1] = packed[0], packed[1]
    PB[1, 0], PB[1, 1] = roll(packed[2], 8), roll(packed[3], 8)

    def pair(x, rows):
        l = lanes(rows)
        return gat(x, (2 * l) & 127) + gat(x, (2 * l + 1) & 127)

    l16 = lanes(16)

    def down1(x, c):
        out = []
        for n in range(2):
            a, b = (E0[n, 7 + 2 * x + p, pl.ds(8, 16, stride=2)] + E0[n, 7 + 2 * x + p, pl.ds(9, 16, stride=2)] for p in range(2))
            t = a + b
            out.append(pair(t, 16))
        rk = jnp.where(l16 < 64, out[0], 0.125 * out[1])
        E1[7 + x, 8:24] = rk
        here = ((l16 & 63) >> 3) == x
        return (
            jnp.where(here, roll(rk, 8 * x), c[0]),
            jnp.where(here, roll(rk, (8 * x + 72) & 127), c[1]),
        )

    zero16 = jnp.zeros((16, 128), f32)
    low1 = high1 = zero16
    for x in range(8):
        low1, high1 = down1(x, (low1, high1))
    for side, val in enumerate((low1, high1)):
        PB[side, 2, 0:8] = val[0:8]
        PB[side, 2, 24:32] = val[8:16]

    l8 = lanes(8)
    zero8 = jnp.zeros((8, 128), f32)

    def down2(x, c):
        def part(p, n):
            return E1[7 + 2 * x + p, pl.ds(8 + n, 8, stride=2)]

        t = (part(0, 0) + part(0, 1)) + (part(1, 0) + part(1, 1))
        rk = pair(t, 8)
        rk = jnp.where(((l8 >> 5) & 1) == 1, 0.125 * rk, rk)
        RK2[x] = rk
        here, edge = (l8 >> 5) == x, (l8 < 64) & (((l8 & 31) >> 3) == x)
        return (
            jnp.where(here, roll(rk, 32 * x), c[0]),
            jnp.where(here, roll(rk, (32 * x + 96) & 127), c[1]),
            jnp.where(edge, roll(rk, 8 * x), c[2]),
            jnp.where(edge, roll(rk, (8 * x + 104) & 127), c[3]),
        )

    r2 = k2 = low2 = high2 = zero8
    for x in range(4):
        r2, k2, low2, high2 = down2(x, (r2, k2, low2, high2))
    l4 = lanes(4)
    rk3 = []
    for x in range(2):
        t = (RK2[2 * x, pl.ds(0, 4, stride=2)] + RK2[2 * x, pl.ds(1, 4, stride=2)]) + (
            RK2[2 * x + 1, pl.ds(0, 4, stride=2)] + RK2[2 * x + 1, pl.ds(1, 4, stride=2)]
        )
        T[x, 0:4], T[x, 4:8] = t, t
        t = pair(T[x, 0:8], 8)
        rk3.append(jnp.where(((l8 >> 4) & 1) == 1, 0.125 * t, t))
    m3 = jnp.where(((l8 >> 5) & 1) == 0, rk3[0], rk3[1])
    E23[gy, gx, 0], E23[gy, gx, 1] = r2, k2
    RK2[0] = jnp.where(l8 < 64, low2, m3)
    RK2[1] = jnp.where(l8 < 64, high2, m3)

    for L in (L0, LS, L1, L2, L3, L4):
        L.clear()

    def sides(at, n):
        return jnp.where(at > 0, 1, 0) + jnp.where(at < n - 1, 1, 0)

    pl.semaphore_wait(bar, 10 + sides(gx, 4) * sides(gy, 8) + sides(gz, 8))

    def zcopies(side):
        dev = {"gz": gz - 1 if side == 0 else gz + 1}
        land = 1 - side
        pieces = [
            (RK2.at[side], CB.at[land]),
            (PB.at[side, 2, 0:8], XB.at[1, land, 2, 8:16]),
            (PB.at[side, 2, 24:32], XB.at[1, land, 2, 32:40]),
            (PB.at[side, 0:2], XB.at[1, land, 0:2, 8:40]),
        ]
        return [
            pltpu.make_async_remote_copy(
                src_ref=src, dst_ref=dst, send_sem=bs.at[side, n], recv_sem=br.at[side, n],
                device_id=dev, device_id_type=MESH,
            )
            for n, (src, dst) in enumerate(pieces)
        ]

    def each(cond, copies, what):
        @pl.when(cond)
        def _():
            for c in copies:
                getattr(c, what)()

    zdown, zup = zcopies(0), zcopies(1)
    each(gz > 0, zdown, "start")
    each(gz < 7, zup, "start")

    SRC0X, DST0X = {-1: (7, 14), 0: (7, 23), 1: (16, 23)}, {-1: (23, 30), 0: (7, 23), 1: (0, 7)}
    SRC0Y, DST0Y = {-1: (8, 16), 0: (8, 40), 1: (32, 40)}, {-1: (40, 48), 0: (8, 40), 1: (0, 8)}
    SRC1X, DST1X = {-1: (7, 14), 0: (7, 15), 1: (8, 15)}, {-1: (15, 22), 0: (7, 15), 1: (0, 7)}
    SRC1Y, DST1Y = {-1: (8, 16), 0: (8, 24), 1: (16, 24)}, {-1: (24, 32), 0: (8, 24), 1: (0, 8)}

    def sl(pairs):
        return pl.ds(pairs[0], pairs[1] - pairs[0])

    def near_copies(make):
        return [(inside(dx, dy), inside(-dx, -dy), make(n, dx, dy)) for n, (dx, dy) in enumerate(NEAR)]

    def rc(src, dst, ss, rs, dev):
        return pltpu.make_async_remote_copy(
            src_ref=src, dst_ref=dst, send_sem=ss, recv_sem=rs, device_id=dev, device_id_type=MESH
        )

    def dev_near(dx, dy):
        return {"gx": gx + dx, "gy": gy + dy}

    def thinner(pairs, dx, dy):
        if dx == 0 or dy == 0:
            return sl(pairs)
        return sl((pairs[0] + 1, pairs[1])) if dx == 1 else sl((pairs[0], pairs[1] - 1))

    def planes(pairs, dx, dy, arr):
        cut = (abs(dx) if arr == 0 else 0) + abs(dx * dy)
        return sl((pairs[0] + cut, pairs[1])) if dx == 1 else sl((pairs[0], pairs[1] - cut))

    def fine(arr):
        return near_copies(lambda n, dx, dy: rc(
            E0.at[arr, planes(SRC0X[dx], dx, dy, arr), sl(SRC0Y[dy])],
            E0.at[arr, planes(DST0X[dx], dx, dy, arr), sl(DST0Y[dy])],
            e0s.at[8 * arr + n], e0r.at[8 * arr + n], dev_near(dx, dy)))

    c0r, c0k = fine(0), fine(1)
    c1 = near_copies(lambda n, dx, dy: rc(
        E1.at[thinner(SRC1X[dx], dx, dy), sl(SRC1Y[dy])], E1.at[thinner(DST1X[dx], dx, dy), sl(DST1Y[dy])], e1s.at[n], e1r.at[n], dev_near(dx, dy)))
    def slab_copies(first, last, base):
        return near_copies(lambda n, dx, dy: rc(
            XB.at[1, :, first:last, sl(SRC0Y[dy])], XB.at[1 - dx, :, first:last, sl(DST0Y[dy])],
            xs.at[base + n], xr.at[base + n], dev_near(dx, dy)))

    cx1, cx0 = slab_copies(2, 3, 0), slab_copies(0, 2, 8)

    gather_x = [
        rc(E23.at[gy, gx], E23.at[gy, gx], gs.at[a - 1], gr.at[a - 1], {"gx": rem(gx + a, 4)}) for a in range(1, 4)
    ]
    gather_y = []
    for b in range(1, 8):
        dev = {"gy": rem(gy + b, 8)}
        wide = rc(E23.at[gy], E23.at[gy], cs.at[b - 1], cr.at[b - 1], dev)
        thin = rc(E23.at[gy, :, 3:4], E23.at[gy, :, 3:4], cs.at[b - 1], cr.at[b - 1], dev)
        up, fromlow = gy + b < 8, gy - b >= 0
        if b == 4:
            gather_y.append((thin, None, None))
        elif b < 4:
            gather_y.append((wide if b == 1 else thin, up, fromlow))
        else:
            gather_y.append((wide if b == 7 else thin, jnp.logical_not(up), jnp.logical_not(fromlow)))

    def each_y(what, end):
        for copy, to, of in gather_y:
            cond = of if end else to
            if cond is None:
                getattr(copy, what)()
            else:
                each(cond, [copy], what)

    for ok, _, c in c1 + [c0k[n] for n in (1, 6, 3, 4, 0, 2, 5, 7)]:
        each(ok, [c], "start")

    @pl.when(gz == 0)
    def _():
        for n in range(3):
            XB[1, 0, n, 8:40] = zero32
        CB[0] = zero8

    @pl.when(gz == 7)
    def _():
        for n in range(3):
            XB[1, 1, n, 8:40] = zero32
        CB[1] = zero8

    each(gz < 7, zdown[0:1], "wait_recv")
    each(gz > 0, zup[0:1], "wait_recv")
    top = rowid(8) < 4
    E23[gy, gx, 2] = jnp.where(l8 < 64, CB[0], roll(CB[1], 64))
    E23[gy, gx, 3] = jnp.where(l8 < 64, m3, jnp.where(top, CB[0], CB[1]))
    for c in gather_x:
        c.start()
    each(gz < 7, zdown[1:3], "wait_recv")
    each(gz > 0, zup[1:3], "wait_recv")
    for ok, _, c in cx1 + [c0r[n] for n in (1, 6, 3, 4, 0, 2, 5, 7)]:
        each(ok, [c], "start")

    for c in gather_x:
        c.wait_recv()
    each_y("start", False)
    each(gz < 7, zdown[3:4], "wait_recv")
    each(gz > 0, zup[3:4], "wait_recv")
    for ok, _, c in cx0:
        each(ok, [c], "start")

    for _, okr, c in c1 + cx1:
        each(okr, [c], "wait_recv")

    l32b = lanes(32)

    def load1(i):
        x = i - 7
        dx = jnp.where(x >= 0, 1, 0) + jnp.where(x >= 8, 1, 0)
        xl = x & 7
        m = mask1(i)
        main = E1[i]
        out1 = []
        lo = jnp.concatenate([XB[dx, 0, 2, 0:16], XB[dx, 0, 2, 32:48]], axis=0)
        hi = jnp.concatenate([XB[dx, 1, 2, 0:16], XB[dx, 1, 2, 32:48]], axis=0)
        for isk in range(2):
            at = 8 * xl + 64 * isk
            mid = roll(main, 64) if isk else main
            out = jnp.where(
                l32b < 64, mid,
                jnp.where(l32b < 96, roll(hi, (192 - at) & 127), roll(lo, (248 - at) & 127)),
            )
            out = jnp.where(m, out, 0.0)
            if isk:
                out1.append((L1.K, (i, slice(8, 40)), out))
            else:
                out1.append((L1.R, i, out))
        return out1

    loop(0, 22, 4, load1)
    L1.build()
    L1.smooth6()

    for _, okr, c in c0k:
        each(okr, [c], "wait_recv")
    loop(0, 30, 6, lambda i: [(L0.K, (i, slice(8, 56)), jnp.where(mask0(i), E0[1, i], 0.0))])
    L0.build(start=False)
    for _, okr, c in c0r:
        each(okr, [c], "wait_recv")

    def load0(i):
        r = jnp.where(mask0(i), E0[0, i], 0.0)
        return [(L0.R, i, r), (L0.VA, (i, slice(8, 56)), B0 * (r * L0.ID[i]))]

    loop(1, 29, 7, load0)
    L0.smooth6()

    for _, okr, c in cx0:
        each(okr, [c], "wait_recv")
    ls, gsl, zz = group(48)

    def load_slab(xi):
        m = masks(xi + 1)
        x = 10 * gsl + (xi - 7)
        which = jnp.where(x >= 0, 1, 0) + jnp.where(x >= 16, 1, 0)
        xl = x & 15
        ilo = (8 * xl + zz) & 127
        ihi = (8 * xl + zz - 34) & 127
        imain = jnp.where(zz < 21, zz - 8, zz + 94) & 127
        outs = []
        for arr in range(2):
            src = L0.K if arr else L0.R
            parts = []
            for g in range(3):
                plane = src[10 * g + xi, 8:56] if arr else src[10 * g + xi]
                parts.append(gat(plane, imain))
            mid = jnp.where(gsl == 0, parts[0], jnp.where(gsl == 1, parts[1], parts[2]))
            lo = [gat(XB[d, 0, arr], ilo) for d in range(3)]
            hi = [gat(XB[d, 1, arr], ihi) for d in range(3)]
            pick = [jnp.where(which == 0, t[0], jnp.where(which == 1, t[1], t[2])) for t in (lo, hi)]
            out = jnp.where(zz < 8, pick[0], jnp.where(zz >= 34, pick[1], mid))
            out = jnp.where(m, out, 0.0)
            if arr:
                outs.append((LS.K, (1 + xi, slice(8, 56)), out))
            else:
                outs.append((LS.R, 1 + xi, out))
        return outs

    loop(0, 10, 2, load_slab)

    def ghosts(ref):
        ref[0, 8:56] = roll(ref[10, 8:56], 42)
        ref[11, 8:56] = roll(ref[1, 8:56], 86)

    ghosts(LS.K)
    LS.build()
    ghosts(LS.VA)
    LS.smooth6(after=ghosts, trim=False)

    each_y("wait_recv", True)
    in3 = yz(8, 0, 8, 16, 16, 16)
    for sx in range(4):
        def load3(q, sx=sx):
            a, b = E23[2 * q, sx, 3], E23[2 * q + 1, sx, 3]
            m = jnp.where(top, a, b)
            lo = jnp.where(top, a, pltpu.roll(b, 4, 0))
            hi = jnp.where(top, pltpu.roll(a, 4, 0), b)
            out3 = []
            for xl in range(2):
                for isk in range(2):
                    at = 32 * xl + 16 * isk
                    out = jnp.where(
                        l8 < 16, roll(m, (128 - at) % 128),
                        jnp.where(l8 < 32, roll(hi, (16 - 64 - at) % 128), roll(lo, (112 - 64 - at) % 128)),
                    )
                    out = jnp.where(in3, out, 0.0)
                    plane = 1 + 2 * sx + xl
                    if isk:
                        out3.append((L3.K, (plane, slice(8 + 8 * q, 16 + 8 * q)), out))
                    else:
                        out3.append((L3.R, (plane, slice(8 * q, 8 * q + 8)), out))
            return out3

        loop(0, 4, 4, load3)
    L3.build()
    L3.step(L3.VA, L3.VB, A1, B1, 0, True)

    def residue(i):
        _, av = L3.flux(L3.VB, i)
        return [(RES, i - 1, L3.R[i] - av)]

    loop(1, 9, 4, residue)
    in4 = mask4(0)

    def down4(x):
        t = (RES[2 * x, pl.ds(0, 16, stride=2)] + RES[2 * x, pl.ds(1, 16, stride=2)]) + (
            RES[2 * x + 1, pl.ds(0, 16, stride=2)] + RES[2 * x + 1, pl.ds(1, 16, stride=2)]
        )
        r4 = jnp.where(in4, pair(t, 16), 0.0)
        t = (L3.K[1 + 2 * x, pl.ds(8, 16, stride=2)] + L3.K[1 + 2 * x, pl.ds(9, 16, stride=2)]) + (
            L3.K[2 + 2 * x, pl.ds(8, 16, stride=2)] + L3.K[2 + 2 * x, pl.ds(9, 16, stride=2)]
        )
        k4 = jnp.where(in4, 0.125 * pair(t, 16), 0.0)
        return [(L4.R, 1 + x, r4), (L4.K, (1 + x, slice(8, 24)), k4)]

    loop(0, 4, 4, down4)
    L4.build()
    L4.step(L4.VA, L4.VB, A1, B1, 0, True)
    L4.step(L4.VB, L4.VA, A2, B2, 0)
    L4.step(L4.VA, L4.VB, A3, B3, 0)

    def repeat_lanes(x, rows):
        l = lanes(rows)
        return gat(x, jnp.where(l < 96, l >> 1, (l >> 1) + 64))

    def repeat_rows(ref, slot, x, rows):
        ref[slot, pl.ds(0, rows, stride=2)] = x
        ref[slot, pl.ds(1, rows, stride=2)] = x
        return ref[slot, 0 : 2 * rows]

    def up4(x):
        t = repeat_rows(T, x, repeat_lanes(L4.VB[1 + x, 8:24], 16), 16)
        rows = slice(8, 40)
        return [(L3.VB, (1 + 2 * x + p, rows), L3.VB[1 + 2 * x + p, rows] + t) for p in range(2)]

    loop(0, 4, 4, up4)
    L3.step(L3.VB, L3.VA, 0.0, B0, 0)
    L3.step(L3.VA, L3.VB, A1, B1, 0)

    def load2(i):
        xg = 4 * gx + i - 7 + 8
        sx = (xg >> 2) - 2
        xl = xg & 3
        scx = jnp.clip(sx, 0, 3)
        m = mask2(i)
        out2 = []
        for n in range(3):
            sy = jnp.clip(gy + n - 1, 0, 7)
            r, k, edge = E23[sy, scx, 0], E23[sy, scx, 1], E23[sy, scx, 2]
            mn = m[8 * n : 8 * n + 8]
            for isk, mid in ((0, r), (1, k)):
                at = 8 * xl + 32 * isk
                out = jnp.where(
                    l8 < 32, roll(mid, (128 - 32 * xl) & 127),
                    jnp.where(l8 < 64, roll(edge, (224 - at) & 127), roll(edge, (248 - at) & 127)),
                )
                out = jnp.where(mn, out, 0.0)
                if isk:
                    out2.append((L2.K, (i, slice(8 + 8 * n, 16 + 8 * n)), out))
                else:
                    out2.append((L2.R, (i, slice(8 * n, 8 * n + 8)), out))
        return out2

    loop(0, 18, 6, load2)
    L2.build()
    L2.smooth6()

    def up3(q):
        w = L3.VB[2 * gx + q, pl.ds(4 * gy + 4, 16)]
        t = repeat_rows(T, 4 + q, repeat_lanes(w, 16), 16)[0:24]
        rows = slice(8, 32)
        return [(L2.VB, (2 * q + 5 + p, rows), L2.VB[2 * q + 5 + p, rows] + t) for p in range(2)]

    loop(0, 4, 4, up3)

    def up2(q):
        t = repeat_rows(T, 8 + q, repeat_lanes(L2.VB[q + 6, 12:28], 16), 16)
        rows = slice(8, 40)
        return [(L1.VB, (2 * q + 5 + p, rows), L1.VB[2 * q + 5 + p, rows] + t) for p in range(2)]

    loop(0, 6, 6, up2)

    l48, l24 = lanes(48), lanes(24)

    def merge(q):
        w = L1.VB[q + 6, 12:36]
        t = repeat_rows(T, 14 + q, gat(w, l24 >> 1), 24)
        th = repeat_rows(TH, q, gat(w, jnp.where(l24 == 0, 127, 64)), 24)
        out = []
        for p in range(2):
            i = 2 * q + 5 + p
            g = jnp.where(i >= 10, 1, 0) + jnp.where(i >= 20, 1, 0)
            xi = i - 10 * g
            sv = LS.VB[1 + xi, 8:56]
            sk = LS.K[1 + xi, 8:56]
            off = 42 * g
            v = jnp.where(
                l48 < 6, roll(sv, (248 - off) & 127),
                jnp.where(l48 >= 122, roll(sv, (222 - off) & 127), L0.VB[i, 8:56]),
            )
            hv = jnp.where(l48 < 64, roll(sv, (249 - off) & 127), roll(sv, (221 - off) & 127)) + th
            kh = jnp.where(l48 < 64, roll(sk, (249 - off) & 127), roll(sk, (221 - off) & 127))
            out += [(L0.VB, (i, slice(8, 56)), v + t), (HV, i, hv), (KH, i, kh)]
        return out

    loop(0, 10, 2, merge)

    def final(x):
        i = x + 7
        c = slice(16, 48)
        v = L0.VB[i, c]
        k = L0.K[i, c]
        hv, kh = HV[i, 8:40], KH[i, 8:40]
        out = L0.CX[i, 8:40] * (v - L0.VB[i - 1, c])
        out = out + L0.CX[i + 1, 8:40] * (v - L0.VB[i + 1, c])
        out = out + L0.CY[i, 8:40] * (v - L0.VB[i, 15:47])
        out = out + L0.CY[i, 9:41] * (v - L0.VB[i, 17:49])
        cl = 0.5 * (k + jnp.where(l32 == 0, kh, roll(k, 1)))
        cr = 0.5 * (k + jnp.where(l32 == 127, kh, roll(k, 127)))
        out = out + cl * (v - jnp.where(l32 == 0, hv, roll(v, 1)))
        out = out + cr * (v - jnp.where(l32 == 127, hv, roll(v, 127)))
        return [(corr_out, x, v), (res_out, x, E0[0, i, 8:40] - out)]

    loop(0, 16, 4, final)

    each(gz > 0, zdown, "wait_send")
    each(gz < 7, zup, "wait_send")
    for ok, _, c in c0r + c0k + c1 + cx0 + cx1:
        each(ok, [c], "wait_send")
    for c in gather_x:
        c.wait_send()
    each_y("wait_send", False)


def level_scratch(X, Y):
    big, mid = pltpu.VMEM((X, Y + 16, 128), f32), pltpu.VMEM((X, Y, 128), f32)
    return [big, mid, mid, pltpu.VMEM((X, Y + 8, 128), f32), mid, mid, mid, big, big]


def shards(source, conductivity):
    dma = pltpu.SemaphoreType.DMA
    vm = lambda *shape: pltpu.VMEM(shape, f32)
    out = jax.ShapeDtypeStruct((16, 32, 128), f32)
    scratch = [
        vm(2, 30, 48, 128), vm(22, 32, 128), vm(8, 4, 4, 8, 128), vm(3, 2, 3, 48, 128), vm(2, 3, 32, 128),
        vm(4, 8, 128), vm(2, 8, 128), vm(24, 48, 128), vm(10, 48, 128), vm(8, 32, 128), vm(30, 48, 128), vm(30, 48, 128),
        dma((2,)), dma((16,)), dma((16,)), dma((8,)), dma((8,)), dma((3,)), dma((3,)), dma((2, 4)), dma((2, 4)),
        dma((16,)), dma((16,)), dma((7,)), dma((7,)),
    ]
    for X, Y in ((30, 48), (12, 48), (22, 32), (18, 24), (10, 32), (6, 16)):
        scratch += level_scratch(X, Y)
    return pl.pallas_call(
        kernel,
        out_shape=(out, out),
        in_specs=[pl.BlockSpec(memory_space=pltpu.HBM)] * 2,
        out_specs=(pl.BlockSpec(memory_space=pltpu.VMEM),) * 2,
        scratch_shapes=scratch,
        compiler_params=pltpu.CompilerParams(
            collective_id=0, has_side_effects=True, vmem_limit_bytes=48 * 1024 * 1024
        ),
        name="multigrid",
    )(source, conductivity)


def solution(mesh):
    spec = P("gx", "gy", "gz")
    return jax.shard_map(shards, mesh=mesh, in_specs=(spec, spec), out_specs=(spec, spec), check_vma=False)
```
